128 devices in a mesh: front: 4 (over z_hi, core), tile: 32 (over z_lo, y, x).
Axes of the slice: x: 4, y: 4, z: 4 (z_hi: 2, z_lo: 2; z = z_hi * 2 + z_lo), core: 2. Of those that a mesh axis runs over, the one named last changes fastest.
Arguments:
- fronts: float32 [4, 32, 2048, 1024], P('front', 'tile')
- parents: bfloat16 [4, 32, 2048, 1024], P('front', 'tile'), may hold values from -3 to 3
- parent_of: int32 [4], replicated, may hold values from 0 to 3
- block_map: int32 [4, 48], replicated, may hold values from 0 to 63, as said below
Outputs:
- factor: bfloat16 [4, 32, 2048, 256], P('front', 'tile')
- merged: float32 [4, 32, 2048, 1024], P('front', 'tile')
The draws below stay inside these ranges and needn't reach their ends.
Inputs may be any that keep to these rules, and one draw needn't show every extreme that they name: block_map[g, a] % 8 == a % 8, and the 48 entries of one front are distinct.
All inputs are finite; a program needn't handle non-finite values.
Results may differ from the reference program's by a relative error of at most 0.0032.
Values may be sent and summed in bfloat16 or wider, within the bound.
No kernel may reach another device: no remote copies, remote signals or barrier semaphores. Data moves between devices by JAX's collectives and lax.ppermute only.
A program may use at most 192 MiB of HBM per device.

```python
import jax
import jax.numpy as jnp
from jax import lax

F = 8192
BLK = 128
NPAN = 2
NFRONT = 4
GROW = 4
PW = 1024
NP = 2048
TR = 2048
TC = 1024
NCB = 48
NPB = 64
N_TILE = 32


def draw_fronts(key, part):
    key = jax.random.fold_in(key, 11)
    factor_key = jax.random.fold_in(key, 0)
    rank_width = max(F // 2, 2 * NP)
    factor_rows = jax.random.normal(factor_key, (NFRONT, F, rank_width), jnp.float32)
    product = jnp.einsum('gik,gjk->gij', factor_rows, factor_rows, precision=lax.Precision.HIGHEST) * (1.0 / rank_width)
    symmetric = 0.5 * (product + jnp.swapaxes(product, 1, 2))
    full_matrix = symmetric + 0.25 * jnp.eye(F, dtype=jnp.float32)[None]
    grid = full_matrix.reshape(NFRONT, TR // BLK, GROW, BLK, TC // BLK, 8, BLK)
    grid = jnp.roll(grid.transpose(0, 2, 5, 1, 3, 4, 6), 1, axis=1)
    return grid.reshape(NFRONT, GROW * 8, TR, TC)


def draw_block_map(key, part):
    key = jax.random.fold_in(key, 23)
    slots = NPB // 8
    keep_count = NCB // 8
    key_list = jax.random.split(key, NFRONT * 8)
    orders = jax.vmap(lambda one_key: jax.random.permutation(one_key, slots))(key_list)
    places = jnp.argsort(orders, axis=1)
    values = jnp.arange(slots)[None, :]
    row_ids = jnp.arange(NFRONT * 8)[:, None]
    scores = jnp.where((row_ids == 7) & (values == slots - 1), -2, jnp.where((row_ids == 0) & (values == 0), -1, places))
    chosen = jnp.argsort(scores, axis=1)[:, :keep_count]
    chosen = chosen.reshape(NFRONT, 8, keep_count).transpose(0, 2, 1)
    residue = jnp.arange(8)[None, None, :]
    return (chosen * 8 + residue).reshape(NFRONT, NCB).astype(jnp.int32)


def place_ends(values, stream_key, low, top_value):
    longest = values.shape.index(max(values.shape))
    spots = []
    for shift in (0, 1):
        where = [jax.random.randint(jax.random.fold_in(stream_key, axis), (), 0, length) for axis, length in enumerate(values.shape)]
        where[longest] = (where[longest] + shift) % values.shape[longest]
        spots.append(tuple(where))
    return values.at[spots[0]].set(low).at[spots[1]].set(top_value)


def steps_of(key, shape, pieces, least, high):
    loudness = 1.0
    for axis_at, blocks in pieces:
        heights = jax.random.uniform(jax.random.fold_in(jax.random.fold_in(key, 6), axis_at), (blocks,), jnp.float32, least / len(pieces), high / len(pieces))
        loudness = loudness * jnp.repeat(jnp.exp(heights), shape[axis_at] // blocks).reshape((-1,) + (1,) * (len(shape) - 1 - axis_at))
    return loudness


def normal_values(key, shape, spread, bound, cuts=(), kind=jnp.bfloat16):
    array = spread * jax.random.normal(key, shape, jnp.float32)
    if cuts:
        array = array * steps_of(key, shape, cuts, -0.22, 0.18)
    return jnp.clip(array, -bound, bound).astype(kind)


def setup_inputs(seed: int = 0) -> dict:
    seeds = jax.random.split(jax.random.key(seed), 5)
    fronts = draw_fronts(jax.random.fold_in(seeds[4], 71), 0)
    parents = normal_values(seeds[1], (NFRONT, N_TILE, TR, TC), 0.5, 3.0, ((0, 4), (1, 32)))
    parent_of = place_ends(jax.random.randint(seeds[2], (NFRONT,), 0, NFRONT), jax.random.fold_in(seeds[2], 1), 0, NFRONT - 1).astype(jnp.int32)
    block_map = draw_block_map(jax.random.fold_in(seeds[4], 71), 0)
    return {"fronts": fronts, "parents": parents, "parent_of": parent_of, "block_map": block_map}


def to_full(tiles):
    grid = tiles.reshape(GROW, 8, TR // BLK, BLK, TC // BLK, BLK)
    grid = jnp.roll(grid, -1, axis=0)
    return grid.transpose(2, 0, 3, 4, 1, 5).reshape(F, F)

def to_tiles(full_matrix, columns):
    grid = full_matrix.reshape(TR // BLK, GROW, BLK, columns // (8 * BLK), 8, BLK)
    grid = jnp.roll(grid.transpose(1, 4, 0, 2, 3, 5), 1, axis=0)
    return grid.reshape(GROW * 8, TR, columns // 8)

def factor_front(tiles):
    full_matrix = to_full(tiles)
    identity = jnp.eye(PW, dtype=jnp.float32)
    column_list = []
    for panel_step in range(NPAN):
        low_edge = panel_step * PW
        high_edge = low_edge + PW
        lower_factor = jnp.linalg.cholesky(full_matrix[low_edge:high_edge, low_edge:high_edge])
        inverse = lax.linalg.triangular_solve(lower_factor, identity, left_side=True, lower=True)
        panel_vals = jnp.dot(full_matrix[low_edge:, low_edge:high_edge].astype(jnp.float32), inverse.T.astype(jnp.float32), precision=lax.Precision.HIGHEST, preferred_element_type=jnp.float32).astype(jnp.bfloat16)
        column_list.append(jnp.concatenate([jnp.zeros((low_edge, PW), jnp.bfloat16), panel_vals], 0))
        trailing = panel_vals[PW:]
        update = jnp.dot(trailing.astype(jnp.float32), trailing.T.astype(jnp.float32), preferred_element_type=jnp.float32)
        full_matrix = full_matrix.at[high_edge:, high_edge:].add(-update)
    factor_full = jnp.concatenate(column_list, 1)
    contribution = full_matrix[NP:, NP:].astype(jnp.bfloat16)
    return (to_tiles(factor_full, NP), contribution)

def reference(fronts, parents, parent_of, block_map):
    factor_list = []
    contribution_list = []
    for front_no in range(NFRONT):
        factor_tiles, contribution = factor_front(fronts[front_no])
        factor_list.append(factor_tiles)
        contribution_list.append(contribution)
    merged_list = []
    for group_no in range(NFRONT):
        accum = to_full(parents[group_no].astype(jnp.float32)).reshape(NPB, BLK, NPB, BLK)
        for front_no in range(NFRONT):
            weight = (parent_of[front_no] == group_no).astype(jnp.float32)
            blocks = contribution_list[front_no].astype(jnp.float32).reshape(NCB, BLK, NCB, BLK).transpose(0, 2, 1, 3)
            mapping = block_map[front_no]
            accum = accum.at[mapping[:, None], :, mapping[None, :], :].add(weight * blocks)
        merged_list.append(to_tiles(accum.reshape(F, F), F))
    return (jnp.stack(factor_list), jnp.stack(merged_list))
```

```python
import functools

import jax
import jax.numpy as jnp
from jax import lax
from jax.experimental import pallas as pl
from jax.experimental.pallas import tpu as pltpu
from jax.sharding import PartitionSpec as P

BLK = 128
F32 = jnp.float32
BF16 = jnp.bfloat16
NN = (((1,), (0,)), ((), ()))
NT = (((1,), (1,)), ((), ()))


def dot(a, b, dims):
    return lax.dot_general(a, b, dims, preferred_element_type=F32)


def dot_exact(a, b, dims):
    return lax.dot_general(a, b, dims, precision=lax.Precision.HIGHEST, preferred_element_type=F32)


def split(x):
    hi = x.astype(BF16)
    return hi, (x - hi.astype(F32)).astype(BF16)


def dot3(a, b, dims):
    return dot(a[0], b[0], dims) + (dot(a[0], b[1], dims) + dot(a[1], b[0], dims))


def lane_of(x, lane):
    return jnp.broadcast_to(x[:, lane : lane + 1], (8, BLK))


def row_of(x, row):
    return jnp.broadcast_to(x[row : row + 1, :], (8, BLK))


def factor_block(rows, out_ref, out_row, out_col):
    S = list(rows)
    lanes = lax.broadcasted_iota(jnp.int32, (8, BLK), 1)
    subs = lax.broadcasted_iota(jnp.int32, (8, BLK), 0)
    G = [(lanes == subs + 8 * v).astype(F32) for v in range(16)]
    for v0 in range(16):
        C = {v: [lane_of(S[v], 8 * v0 + j) for j in range(8)] for v in range(v0, 16)}
        d = [[row_of(C[v0][j], i) if i >= j else None for j in range(8)] for i in range(8)]
        Rs = [row_of(S[v0], i) for i in range(8)]
        Rg = [row_of(G[v0], i) for i in range(8)]
        Cn = list(C[v0 + 1]) if v0 < 15 else None
        m = [[None] * 8 for _ in range(8)]
        Us, Ug = [None] * 8, [None] * 8
        wrows = None
        for j in range(8):
            rs = lax.rsqrt(d[j][j])
            p = rs * rs
            w = Rg[j] * rs
            wrows = w if j == 0 else jnp.where(subs == j, w, wrows)
            for i in range(j + 1, 8):
                m[i][j] = d[i][j] * p
            for i in range(j + 1, 8):
                for k in range(j + 1, i + 1):
                    d[i][k] = d[i][k] - m[i][j] * d[k][j]
            Us[j] = Rs[j] * p
            Ug[j] = Rg[j] * p
            if Cn is not None:
                S[v0 + 1] = S[v0 + 1] - Cn[j] * Us[j]
                G[v0 + 1] = G[v0 + 1] - Cn[j] * Ug[j]
            for i in range(j + 1, 8):
                Rs[i] = Rs[i] - m[i][j] * Rs[j]
                Rg[i] = Rg[i] - m[i][j] * Rg[j]
                if Cn is not None:
                    Cn[i] = Cn[i] - m[i][j] * Cn[j]
        out_ref[pl.ds(out_row + 8 * v0, 8), pl.ds(out_col, BLK)] = wrows
        if v0 < 14:
            for j in range(6, -1, -1):
                for i in range(j + 1, 8):
                    Us[j] = Us[j] - m[i][j] * Us[i]
                    Ug[j] = Ug[j] - m[i][j] * Ug[i]
            for v in range(v0 + 2, 16):
                for j in range(8):
                    S[v] = S[v] - C[v][j] * Us[j]
                    G[v] = G[v] - C[v][j] * Ug[j]


def chol_inverse(A, W, Ls):
    W[...] = jnp.zeros(W.shape, F32)

    def step(kb, _):
        r0 = pl.multiple_of(kb * BLK, BLK)
        rows = [A[pl.ds(pl.multiple_of(r0 + 8 * v, 8), 8), pl.ds(r0, BLK)] for v in range(16)]
        factor_block(rows, W, r0, r0)

        @pl.when(kb % 2 == 0)
        def _():
            r1 = pl.multiple_of(r0 + BLK, BLK)
            wkk = W[pl.ds(r0, BLK), pl.ds(r0, BLK)]
            low = dot_exact(A[pl.ds(r1, BLK), pl.ds(r0, BLK)], wkk, NT)
            Ls[...] = low
            A[pl.ds(r1, BLK), pl.ds(r1, BLK)] -= dot_exact(low, low, NT)

        @pl.when(kb % 2 == 1)
        def _():
            q = pl.multiple_of(r0 - BLK, BLK)
            t = dot_exact(Ls[...], W[pl.ds(q, BLK), pl.ds(q, BLK)], NN)
            W[pl.ds(r0, BLK), pl.ds(q, BLK)] = -dot_exact(W[pl.ds(r0, BLK), pl.ds(r0, BLK)], t, NN)

        for c in range(4):
            @pl.when(kb == 2 * c + 1)
            def _():
                lo, hi = 256 * c, 256 * (c + 1)
                wd = W[lo:hi, lo:hi]
                if c > 0:
                    W[lo:hi, :lo] = dot_exact(wd, W[lo:hi, :lo], NN)
                if c < 3:
                    low = dot_exact(A[hi:, lo:hi], wd, NT)
                    for n in range(c + 1, 4):
                        a, b = 256 * n, 256 * (n + 1)
                        A[a:, a:b] -= dot_exact(low[a - hi :], low[a - hi : b - hi], NT)
                    W[hi:, lo:hi] = -dot_exact(low, wd, NN)
                    if c > 0:
                        W[hi:, :lo] -= dot_exact(low, W[lo:hi, :lo], NN)

        return 0

    lax.fori_loop(0, 8, step, 0)


VMEM = pl.BlockSpec(memory_space=pltpu.VMEM)
PARAMS = pltpu.CompilerParams(vmem_limit_bytes=56 * 2**20)


def cost(flops, data):
    return pl.CostEstimate(flops=flops, bytes_accessed=data, transcendentals=0)


def position():
    tile = lax.axis_index("tile")
    return tile // 8, tile % 8


def times_inverse_t(x, w, put):
    for n in range(4):
        a, b = 256 * n, 256 * (n + 1)
        put(n, dot3((x[0][:, :b], x[1][:, :b]), (w[0][a:b, :b], w[1][a:b, :b]), NT))


def inverse_times(w, x, put):
    for n in range(4):
        a, b = 256 * n, 256 * (n + 1)
        put(n, dot3((w[0][a:b, :b], w[1][a:b, :b]), (x[0][:b], x[1][:b]), NN))


def store_split(hi, lo, index, x):
    h, l = split(x)
    hi[index] = h
    lo[index] = l


def own_columns(left, W, row, col, out, at):
    wc = W[pl.ds(pl.multiple_of(col * BLK, BLK), BLK), :]
    own = dot_exact(left, wc, NT)
    for m in range(2):
        keep = 4 * m + (row + 3) % 4 >= col
        out[m * BLK : (m + 1) * BLK, at : at + BLK] = jnp.where(keep, own[m * BLK : (m + 1) * BLK], 0.0).astype(BF16)


def first_kernel(g, whi, wlo, top, A, W, Ls):
    row, col = position()
    for i in range(8):
        for j in range(8):
            A[i * BLK : (i + 1) * BLK, j * BLK : (j + 1) * BLK] = g[8 * ((i + 1) % 4) + j, (i // 4) * BLK : (i // 4 + 1) * BLK, :]
    chol_inverse(A, W, Ls)
    store_split(whi, wlo, ..., W[...])
    top[...] = jnp.zeros(top.shape, BF16)
    left = jnp.concatenate([g[8 * row + j] for j in range(8)], 1)
    own_columns(left, W, row, col, top, 0)


def second_kernel(g, w0hi, w0lo, low, whi, wlo, top, A, W, Ls, xhi, xlo, keep):
    row, col = position()
    for i in range(8):
        for j in range(8):
            src = g[8 * ((i + 1) % 4) + j, (i // 4) * BLK : (i // 4 + 1) * BLK, :]
            at = slice(i * BLK, (i + 1) * BLK), slice(j * BLK, (j + 1) * BLK)
            store_split(xhi, xlo, at, src[:, :BLK])
            A[at] = src[:, BLK:]

    def put(n, x):
        low[:, 256 * n : 256 * (n + 1)] = x.astype(BF16)

    times_inverse_t((xhi, xlo), (w0hi, w0lo), put)
    for n in range(4):
        a, b = 256 * n, 256 * (n + 1)
        A[a:, a:b] -= dot(low[a:, :], low[a:b, :], NT)
    for m in range(2):
        at = pl.multiple_of((4 * m + (row + 3) % 4) * BLK, BLK)
        keep[m * BLK : (m + 1) * BLK, :] = A[pl.ds(at, BLK), :]
        top[m * BLK : (m + 1) * BLK, :BLK] = low[pl.ds(at, BLK), pl.ds(pl.multiple_of(col * BLK, BLK), BLK)]
    chol_inverse(A, W, Ls)
    store_split(whi, wlo, ..., W[...])
    own_columns(keep[...], W, row, col, top, BLK)


def rows_kernel(panel, *refs):
    pieces, refs = refs[:8], refs[8:]
    row, col = position()
    if panel == 0:
        whi, wlo, out, x = refs
    else:
        whi, wlo, low, first, out, x = refs
    for k in range(8):
        x[:, pl.ds(pl.multiple_of((col ^ k) * BLK, BLK), BLK)] = pieces[k][:, panel * BLK : (panel + 1) * BLK]
    v = x[...]
    if panel == 1:
        v = v - dot(first[...], low[...], NT)

    def put(n, y):
        out[:, 256 * n : 256 * (n + 1)] = y.astype(BF16)

    times_inverse_t(split(v), (whi, wlo), put)


def columns_kernel(*refs):
    pieces = refs[:4]
    w0hi, w0lo, w1hi, w1lo, low, t0, t1, xhi, xlo, y = refs[4:]
    row, _ = position()
    for k in range(4):
        place = ((row ^ k) + 3) % 4
        for m in range(4):
            src = pieces[k][m * BLK : (m + 1) * BLK, :]
            at = pl.ds(pl.multiple_of((4 * (m % 2) + place) * BLK, BLK), BLK)
            if m < 2:
                store_split(xhi, xlo, (at, slice(None)), src)
            else:
                y[at, :] = src

    def put(t):
        def go(n, v):
            t[256 * n : 256 * (n + 1), :] = v.astype(BF16)

        return go

    inverse_times((w0hi, w0lo), (xhi, xlo), put(t0))
    for n in range(4):
        at = slice(256 * n, 256 * (n + 1)), slice(None)
        store_split(xhi, xlo, at, y[at] - dot(low[at], t0[...], NN))
    inverse_times((w1hi, w1lo), (xhi, xlo), put(t1))


def update_kernel(l0, l1, t0, t1, a, out, factor):
    _, col = position()
    out[...] = (a[...] - (dot(l0[...], t0[...], NN) + dot(l1[...], t1[...], NN))).astype(BF16)

    @pl.when(pl.program_id(1) == 0)
    def _():
        at = pl.ds(pl.multiple_of(col * BLK, BLK), BLK)
        factor[:, :BLK] = l0[:, at]
        factor[:, BLK:] = l1[:, at]


def merge_kernel(rows, cols, parent, *refs):
    blocks, out = refs[:4], refs[4]
    i = pl.program_id(0)
    out[...] = parent[...].astype(F32)
    for g in range(4):
        @pl.when(rows[g, i] >= 0)
        def _():
            for j in range(8):
                b = cols[g, j]

                @pl.when(b >= 0)
                def _():
                    at = pl.ds(pl.multiple_of(b * BLK, BLK), BLK)
                    out[:, j * BLK : (j + 1) * BLK] += blocks[g][0, :, at].astype(F32)


def per_device(fronts, parents, parent_of, block_map):
    tile = lax.axis_index("tile")
    row, col = tile // 8, tile % 8
    my_front = lax.axis_index("front")
    a = fronts[0, 0]
    big = jax.ShapeDtypeStruct((1024, 1024), BF16)
    square = pltpu.VMEM((1024, 1024), F32)
    half = pltpu.VMEM((1024, 1024), BF16)
    block = pltpu.VMEM((BLK, BLK), F32)
    top_shape = jax.ShapeDtypeStruct((256, 256), BF16)

    place_r = jnp.arange(12) * 4 + (row + 3) % 4
    place_c = jnp.arange(6) * 8 + col
    at_rows = block_map[:, place_r] // 4
    at_cols = block_map[:, place_c] // 8
    mine = (parent_of == my_front)[:, None]
    hit_r = (at_rows[:, :, None] == jnp.arange(16)) & mine[:, :, None]
    hit_c = at_cols[:, :, None] == jnp.arange(8)
    from_rows = jnp.max(jnp.where(hit_r, jnp.arange(12)[:, None], -1), axis=1).astype(jnp.int32)
    from_cols = jnp.max(jnp.where(hit_c, jnp.arange(6)[:, None], -1), axis=1).astype(jnp.int32)

    g0 = lax.all_gather(a[:256, :BLK], "tile", axis=0)
    g0, a = lax.optimization_barrier((g0, a))
    g1 = lax.all_gather(a[256:512, :256], "tile", axis=0)

    def swap(x, k):
        return lax.ppermute(x, "tile", [(i, i ^ k) for i in range(32)])

    trail = a[512:, :256].reshape(8, 192, 256)
    pieces = [lax.dynamic_index_in_dim(trail, col ^ k, 0, keepdims=False) for k in range(8)]
    pieces = pieces[:1] + [swap(pieces[k], k) for k in range(1, 8)]
    side = a[:512, 256:]
    sides = [side] + [swap(side, 8 * k) for k in range(1, 4)]

    w0hi, w0lo, top0 = pl.pallas_call(
        first_kernel,
        out_shape=(big, big, top_shape),
        in_specs=[VMEM],
        out_specs=(VMEM,) * 3,
        scratch_shapes=[square, square, block],
        compiler_params=PARAMS,
        cost_estimate=cost(50_000_000_000, 8_000_000),
        name="first_panel",
    )(g0)
    first = pl.pallas_call(
        functools.partial(rows_kernel, 0),
        out_shape=jax.ShapeDtypeStruct((192, 1024), BF16),
        in_specs=[VMEM] * 10,
        out_specs=VMEM,
        scratch_shapes=[pltpu.VMEM((192, 1024), F32)],
        compiler_params=PARAMS,
        cost_estimate=cost(1_200_000_000, 6_000_000),
        name="first_rows",
    )(*pieces, w0hi, w0lo)
    groups = [[8 * r + c for c in range(8)] for r in range(4)]
    l0 = lax.all_gather(first, "tile", axis=0, tiled=True, axis_index_groups=groups)
    low, w1hi, w1lo, top1 = pl.pallas_call(
        second_kernel,
        out_shape=(big, big, big, top_shape),
        in_specs=[VMEM] * 3,
        out_specs=(VMEM,) * 4,
        scratch_shapes=[square, square, block, half, half, pltpu.VMEM((256, 1024), F32)],
        compiler_params=PARAMS,
        cost_estimate=cost(60_000_000_000, 16_000_000),
        name="second_panel",
    )(g1, w0hi, w0lo)
    second = pl.pallas_call(
        functools.partial(rows_kernel, 1),
        out_shape=jax.ShapeDtypeStruct((192, 1024), BF16),
        in_specs=[VMEM] * 12,
        out_specs=VMEM,
        scratch_shapes=[pltpu.VMEM((192, 1024), F32)],
        compiler_params=PARAMS,
        cost_estimate=cost(1_700_000_000, 8_000_000),
        name="second_rows",
    )(*pieces, w1hi, w1lo, low, first)
    l1 = lax.all_gather(second, "tile", axis=0, tiled=True, axis_index_groups=groups)
    wide = jax.ShapeDtypeStruct((1024, 768), BF16)
    t0, t1 = pl.pallas_call(
        columns_kernel,
        out_shape=(wide, wide),
        in_specs=[VMEM] * 9,
        out_specs=(VMEM,) * 2,
        scratch_shapes=[pltpu.VMEM((1024, 768), BF16)] * 2 + [pltpu.VMEM((1024, 768), F32)],
        compiler_params=PARAMS,
        cost_estimate=cost(12_000_000_000, 18_000_000),
        name="column_rows",
    )(*sides, w0hi, w0lo, w1hi, w1lo, low)
    contribution, lower = pl.pallas_call(
        update_kernel,
        grid=(3, 3),
        out_shape=(
            jax.ShapeDtypeStruct((1536, 768), BF16),
            jax.ShapeDtypeStruct((1536, 256), BF16),
        ),
        in_specs=[
            pl.BlockSpec((512, 1024), lambda i, j: (i, 0)),
            pl.BlockSpec((512, 1024), lambda i, j: (i, 0)),
            pl.BlockSpec((1024, 256), lambda i, j: (0, j)),
            pl.BlockSpec((1024, 256), lambda i, j: (0, j)),
            pl.BlockSpec((512, 256), lambda i, j: (i + 1, j + 1)),
        ],
        out_specs=(
            pl.BlockSpec((512, 256), lambda i, j: (i, j)),
            pl.BlockSpec((512, 256), lambda i, j: (i, 0)),
        ),
        compiler_params=PARAMS,
        cost_estimate=cost(4_900_000_000, 17_000_000),
        name="update",
    )(l0, l1, t0, t1, a)
    factor = jnp.concatenate([top0, top1, lower], 0)
    arrived = lax.all_gather(contribution, "front", axis=0)

    def child(g):
        return pl.BlockSpec((1, BLK, 768), lambda i, rows, cols: (g, jnp.maximum(rows[g, i], 0), 0))

    merged = pl.pallas_call(
        merge_kernel,
        grid_spec=pltpu.PrefetchScalarGridSpec(
            num_scalar_prefetch=2,
            grid=(16,),
            in_specs=[pl.BlockSpec((BLK, 1024), lambda i, rows, cols: (i, 0))] + [child(g) for g in range(4)],
            out_specs=pl.BlockSpec((BLK, 1024), lambda i, rows, cols: (i, 0)),
        ),
        out_shape=jax.ShapeDtypeStruct((2048, 1024), F32),
        compiler_params=PARAMS,
        cost_estimate=cost(10_000_000, 22_000_000),
        name="merge",
    )(from_rows, from_cols, parents[0, 0], *[arrived] * 4)
    return factor[None, None], merged[None, None]


def solution(mesh):
    return jax.shard_map(
        per_device,
        mesh=mesh,
        in_specs=(P("front", "tile", None, None), P("front", "tile", None, None), P(), P()),
        out_specs=(P("front", "tile", None, None), P("front", "tile", None, None)),
        check_vma=False,
    )
```

```python
import functools

import jax
import jax.numpy as jnp
from jax import lax
from jax.experimental import pallas as pl
from jax.experimental.pallas import tpu as pltpu
from jax.sharding import PartitionSpec as P

BLK = 128
F32 = jnp.float32
BF16 = jnp.bfloat16
NN = (((1,), (0,)), ((), ()))
NT = (((1,), (1,)), ((), ()))


def dot(a, b, dims):
    return lax.dot_general(a, b, dims, preferred_element_type=F32)


def split(x):
    hi = x.astype(BF16)
    return hi, (x - hi.astype(F32)).astype(BF16)


def dot3(a, b, dims):
    return dot(a[0], b[0], dims) + (dot(a[0], b[1], dims) + dot(a[1], b[0], dims))


def dotp(a, b, dims):
    return dot3(split(a), split(b), dims)


def lane_of(x, lane):
    return jnp.broadcast_to(x[:, lane : lane + 1], (8, BLK))


def row_of(x, row):
    return jnp.broadcast_to(x[row : row + 1, :], (8, BLK))


def factor_block(rows, out_ref, out_row, out_col):
    S = list(rows)
    lanes = lax.broadcasted_iota(jnp.int32, (8, BLK), 1)
    subs = lax.broadcasted_iota(jnp.int32, (8, BLK), 0)
    G = [(lanes == subs + 8 * v).astype(F32) for v in range(16)]
    for v0 in range(16):
        C = {v: [lane_of(S[v], 8 * v0 + j) for j in range(8)] for v in range(v0, 16)}
        d = [[row_of(C[v0][j], i) if i >= j else None for j in range(8)] for i in range(8)]
        Rs = [row_of(S[v0], i) for i in range(8)]
        Rg = [row_of(G[v0], i) for i in range(8)]
        Cn = list(C[v0 + 1]) if v0 < 15 else None
        m = [[None] * 8 for _ in range(8)]
        Us, Ug = [None] * 8, [None] * 8
        wrows = None
        for j in range(8):
            rs = lax.rsqrt(d[j][j])
            p = rs * rs
            w = Rg[j] * rs
            wrows = w if j == 0 else jnp.where(subs == j, w, wrows)
            for i in range(j + 1, 8):
                m[i][j] = d[i][j] * p
            for i in range(j + 1, 8):
                for k in range(j + 1, i + 1):
                    d[i][k] = d[i][k] - m[i][j] * d[k][j]
            Us[j] = Rs[j] * p
            Ug[j] = Rg[j] * p
            if Cn is not None:
                S[v0 + 1] = S[v0 + 1] - Cn[j] * Us[j]
                G[v0 + 1] = G[v0 + 1] - Cn[j] * Ug[j]
            for i in range(j + 1, 8):
                Rs[i] = Rs[i] - m[i][j] * Rs[j]
                Rg[i] = Rg[i] - m[i][j] * Rg[j]
                if Cn is not None:
                    Cn[i] = Cn[i] - m[i][j] * Cn[j]
        out_ref[pl.ds(out_row + 8 * v0, 8), pl.ds(out_col, BLK)] = wrows
        if v0 < 14:
            for j in range(6, -1, -1):
                for i in range(j + 1, 8):
                    Us[j] = Us[j] - m[i][j] * Us[i]
                    Ug[j] = Ug[j] - m[i][j] * Ug[i]
            for v in range(v0 + 2, 16):
                for j in range(8):
                    S[v] = S[v] - C[v][j] * Us[j]
                    G[v] = G[v] - C[v][j] * Ug[j]


def chol_inverse(A, W, Ls):
    pairs = A.shape[0] // 256
    W[...] = jnp.zeros(W.shape, F32)

    def step(kb, _):
        r0 = pl.multiple_of(kb * BLK, BLK)
        rows = [A[pl.ds(pl.multiple_of(r0 + 8 * v, 8), 8), pl.ds(r0, BLK)] for v in range(16)]
        factor_block(rows, W, r0, r0)

        @pl.when(kb % 2 == 0)
        def _():
            r1 = pl.multiple_of(r0 + BLK, BLK)
            low = dot3(split(A[pl.ds(r1, BLK), pl.ds(r0, BLK)]), split(W[pl.ds(r0, BLK), pl.ds(r0, BLK)]), NT)
            Ls[...] = low
            low = split(low)
            A[pl.ds(r1, BLK), pl.ds(r1, BLK)] -= dot3(low, low, NT)

        @pl.when(kb % 2 == 1)
        def _():
            q = pl.multiple_of(r0 - BLK, BLK)
            t = dot3(split(Ls[...]), split(W[pl.ds(q, BLK), pl.ds(q, BLK)]), NN)
            W[pl.ds(r0, BLK), pl.ds(q, BLK)] = -dot3(split(W[pl.ds(r0, BLK), pl.ds(r0, BLK)]), split(t), NN)

        for c in range(pairs):
            @pl.when(kb == 2 * c + 1)
            def _():
                lo, hi = 256 * c, 256 * (c + 1)
                wd = split(W[lo:hi, lo:hi])
                if c > 0:
                    W[lo:hi, :lo] = dot3(wd, split(W[lo:hi, :lo]), NN)
                if c < pairs - 1:
                    low = split(dot3(split(A[hi:, lo:hi]), wd, NT))
                    for n in range(c + 1, pairs):
                        a, b = 256 * n, 256 * (n + 1)
                        A[a:, a:b] -= dot3([x[a - hi :] for x in low], [x[a - hi : b - hi] for x in low], NT)
                    W[hi:, lo:hi] = -dot3(low, wd, NN)
                    if c > 0:
                        W[hi:, :lo] -= dot3(low, split(W[lo:hi, :lo]), NN)

        return 0

    lax.fori_loop(0, 2 * pairs, step, 0)


VMEM = pl.BlockSpec(memory_space=pltpu.VMEM)
PARAMS = pltpu.CompilerParams(vmem_limit_bytes=56 * 2**20)


def cost(flops, data):
    return pl.CostEstimate(flops=flops, bytes_accessed=data, transcendentals=0)


def position():
    tile = lax.axis_index("tile")
    return tile // 8, tile % 8


def times_inverse_t(x, w, put):
    for n in range(4):
        a, b = 256 * n, 256 * (n + 1)
        put(n, dot3((x[0][:, :b], x[1][:, :b]), (w[0][a:b, :b], w[1][a:b, :b]), NT))


def inverse_times(w, x, put):
    for n in range(4):
        a, b = 256 * n, 256 * (n + 1)
        put(n, dot3((w[0][a:b, :b], w[1][a:b, :b]), (x[0][:b], x[1][:b]), NN))


def store_split(hi, lo, index, x):
    h, l = split(x)
    hi[index] = h
    lo[index] = l


def block_at(index):
    return pl.ds(pl.multiple_of(index * BLK, BLK), BLK)


def finish_lower(whi, wlo, wa, low, wb):
    first, last = split(wa[...]), split(wb[...])
    below = split(-dot3(last, split(dot3(low, first, NN)), NN))
    for out, d0, d1, x in zip((whi, wlo), first, last, below):
        out[:512, :512] = d0
        out[:512, 512:] = jnp.zeros((512, 512), BF16)
        out[512:, :512] = x
        out[512:, 512:] = d1


def own_part(left, whi, wlo, index):
    return dot3(split(left), (whi[block_at(index), :], wlo[block_at(index), :]), NT)


def kernel_a(*refs):
    pieces = refs[:4]
    wa, top, A, Ls = refs[4:]
    row, col = position()
    here = (row + 3) % 4
    for k in range(4):
        for n in range(4):
            A[block_at(((row ^ n) + 3) % 4), block_at((col % 4) ^ k)] = pieces[k][n * BLK : (n + 1) * BLK, :]
    keep = A[block_at(here), :]
    chol_inverse(A, wa, Ls)
    own = dotp(keep, wa[block_at(col % 4), :], NT)
    top[:, :BLK] = jnp.where((col < 4) & (here >= col), own, 0.0).astype(BF16)
    top[:, BLK:] = jnp.zeros((BLK, BLK), BF16)


def kernel_b(*refs):
    pieces = refs[:4]
    wa, whi, wlo, top, D, A, wb, lhi, llo, keep, Ls = refs[4:]
    row, col = position()
    here = (row + 3) % 4
    for k in range(4):
        for n in range(4):
            at = block_at(((row ^ n) + 3) % 4), block_at((col % 4) ^ k)
            D[at] = pieces[k][n * BLK : (n + 1) * BLK, :BLK]
            A[at] = pieces[k][n * BLK : (n + 1) * BLK, BLK:]
    keep[:, :512] = D[block_at(here), :]
    keep[:, 512:] = A[block_at(here), :]
    low = split(dot3(split(D[...]), split(wa[...]), NT))
    lhi[...], llo[...] = low
    A[...] -= dot3(low, low, NT)
    chol_inverse(A, wb, Ls)
    finish_lower(whi, wlo, wa, (lhi[...], llo[...]), wb)
    own = own_part(keep[...], whi, wlo, col)
    top[:, :BLK] = jnp.where(here + 4 >= col, own, 0.0).astype(BF16)
    top[:, BLK:] = jnp.zeros((BLK, BLK), BF16)


def place(src, i, x, xhi, xlo, blocks):
    rows = block_at(i)
    for half in range(2):
        store_split(xhi, xlo, (rows, block_at(4 * half + x)), src[:, half * BLK : (half + 1) * BLK])
    for n, ref in enumerate(blocks):
        ref[rows, block_at(x)] = src[:, (n + 2) * BLK : (n + 3) * BLK]


def spread(pieces, row, xhi, xlo, blocks):
    for k in range(4):
        for x in range(4):
            place(pieces[k][x], ((row ^ k) + 3) % 4, x, xhi, xlo, blocks)


def kernel_c(*refs):
    pieces = refs[:4]
    w0hi, w0lo, low, wc, top, A, xhi, xlo, keep, Ls = refs[4:]
    row, col = position()
    here = (row + 3) % 4
    for k in range(4):
        for n in range(4):
            place(pieces[k][n * BLK : (n + 1) * BLK, :], ((row ^ n) + 3) % 4, (col % 4) ^ k, xhi, xlo, [A])

    def put(n, x):
        low[:, 256 * n : 256 * (n + 1)] = x.astype(BF16)

    times_inverse_t((xhi, xlo), (w0hi, w0lo), put)
    A[...] -= dot(low[...], low[...], NT)
    keep[...] = A[block_at(here), :]
    chol_inverse(A, wc, Ls)
    own = dotp(keep[...], wc[block_at(col % 4), :], NT)
    top[:, :BLK] = low[block_at(here), block_at(col)]
    top[:, BLK:] = jnp.where((col < 4) & (here >= col), own, 0.0).astype(BF16)


def kernel_d(*refs):
    pieces = refs[:4]
    w0hi, w0lo, lowc, wc, low, whi, wlo, top, D, A, wd, lhi, llo, xhi, xlo, keep, Ls = refs[4:]
    row, col = position()
    here = (row + 3) % 4
    spread(pieces, row, xhi, xlo, [D, A])

    def put(n, x):
        low[:, 256 * n : 256 * (n + 1)] = x.astype(BF16)

    times_inverse_t((xhi, xlo), (w0hi, w0lo), put)
    D[...] -= dot(low[...], lowc[...], NT)
    A[...] -= dot(low[...], low[...], NT)
    keep[:, :512] = D[block_at(here), :]
    keep[:, 512:] = A[block_at(here), :]
    lower = split(dot3(split(D[...]), split(wc[...]), NT))
    lhi[...], llo[...] = lower
    A[...] -= dot3(lower, lower, NT)
    chol_inverse(A, wd, Ls)
    finish_lower(whi, wlo, wc, (lhi[...], llo[...]), wd)
    own = own_part(keep[...], whi, wlo, col)
    top[:, :BLK] = low[block_at(here), block_at(col)]
    top[:, BLK:] = jnp.where(here + 4 >= col, own, 0.0).astype(BF16)


def rows_kernel(panel, *refs):
    pieces, refs = refs[:4], refs[4:]
    row, col = position()
    if panel == 0:
        whi, wlo, out0, out1, x = refs
    else:
        whi, wlo, low_c, low_d, first0, first1, out0, out1, x = refs
    for k in range(4):
        for n in range(2):
            at = (2 * n + panel) * BLK
            x[:, block_at(col ^ k ^ (4 * n))] = pieces[k][:, at : at + BLK]
    v = x[...]
    if panel == 1:
        first = jnp.concatenate([first0[...], first1[...]], 0)
        v = v - jnp.concatenate([dot(first, low[...], NT) for low in (low_c, low_d)], 1)

    def put(n, y):
        out0[:, 256 * n : 256 * (n + 1)] = y[:96].astype(BF16)
        out1[:, 256 * n : 256 * (n + 1)] = y[96:].astype(BF16)

    times_inverse_t(split(v), (whi, wlo), put)


def columns_kernel(top_z, top_y, low_own, low_z, w0hi, w0lo, w1hi, w1lo, low_c, low_d, t0, t1, xhi, xlo, y):
    row, _ = position()
    for n in range(2):
        for top, side in ((top_z, row % 2), (top_y, 1 - row % 2)):
            at = (2 * n + side + 3) % 4
            for m in range(2):
                store_split(xhi, xlo, (block_at(4 * m + at), slice(None)), top[n, m * BLK : (m + 1) * BLK, :])
        for low, flip in ((low_own, n), (low_z, n + 2)):
            at = ((row ^ flip) + 3) % 4
            for m in range(2):
                y[block_at(4 * m + at), :] = low[n, m * BLK : (m + 1) * BLK, :]

    def put(t):
        def go(n, v):
            t[256 * n : 256 * (n + 1), :] = v.astype(BF16)

        return go

    inverse_times((w0hi, w0lo), (xhi, xlo), put(t0))
    for n in range(4):
        at = slice(256 * n, 256 * (n + 1)), slice(None)
        low = (low_c, low_d)[n // 2]
        part = slice(256 * (n % 2), 256 * (n % 2 + 1))
        store_split(xhi, xlo, at, y[at] - dot(low[part, :], t0[...], NN))
    inverse_times((w1hi, w1lo), (xhi, xlo), put(t1))


def update_kernel(l0, l1, t0, t1, a0, a1, a2, out, factor):
    _, col = position()
    total = dot(l0[...], t0[...], NN) + dot(l1[...], t1[...], NN)
    for n, a in enumerate((a0, a1, a2)):
        at = slice(256 * n, 256 * (n + 1))
        out[at, :] = (a[...] - total[at]).astype(BF16)

    @pl.when(pl.program_id(0) == 0)
    def _():
        factor[:, :BLK] = l0[:, block_at(col)]
        factor[:, BLK:] = l1[:, block_at(col)]


def merge_kernel(rows, cols, parent, *refs):
    blocks, out = refs[:8], refs[8]
    i = pl.program_id(0)
    out[...] = parent[...].astype(F32)
    for k in range(4):
        for h in range(2):
            @pl.when((rows[k, i] >= 6 * h) & (rows[k, i] < 6 * h + 6))
            def _():
                for j in range(8):
                    b = cols[k, j]
                    x = blocks[2 * k + h][:, block_at(jnp.maximum(b, 0))].astype(F32)
                    out[:, j * BLK : (j + 1) * BLK] += jnp.where(b >= 0, x, 0.0)


def per_device(fronts, parents, parent_of, block_map):
    tile = lax.axis_index("tile")
    row, col = tile // 8, tile % 8
    my_front = lax.axis_index("front")
    a = fronts[0, 0]
    big = jax.ShapeDtypeStruct((1024, 1024), BF16)
    mid = jax.ShapeDtypeStruct((512, 512), F32)
    wide = jax.ShapeDtypeStruct((512, 1024), BF16)
    top_shape = jax.ShapeDtypeStruct((BLK, 256), BF16)
    piece = pltpu.VMEM((512, 512), BF16)
    quarter = pltpu.VMEM((512, 512), F32)
    strip = pltpu.VMEM((512, 1024), BF16)
    line = pltpu.VMEM((BLK, 1024), F32)
    block = pltpu.VMEM((BLK, BLK), F32)

    place_r = jnp.arange(12) * 4 + (row + 3) % 4
    place_c = jnp.arange(6) * 8 + col
    child = my_front ^ jnp.arange(4)
    child_map = block_map[child]
    at_rows = child_map[:, place_r] // 4
    at_cols = child_map[:, place_c] // 8
    mine = (parent_of[child] == my_front)[:, None]
    crossing = jnp.sum(jnp.where(parent_of // 2 != jnp.arange(4) // 2, 1 << jnp.arange(4), 0))
    hit_r = (at_rows[:, :, None] == jnp.arange(16)) & mine[:, :, None]
    hit_c = at_cols[:, :, None] == jnp.arange(8)
    from_rows = jnp.max(jnp.where(hit_r, jnp.arange(12)[:, None], -1), axis=1).astype(jnp.int32)
    from_cols = jnp.max(jnp.where(hit_c, jnp.arange(6)[:, None], -1), axis=1).astype(jnp.int32)

    def swap(x, k):
        return lax.ppermute(x, "tile", [(i, i ^ k) for i in range(32)])

    def call(kernel, name, flops, ins, outs, scratch):
        return pl.pallas_call(
            kernel,
            out_shape=outs,
            in_specs=[VMEM] * len(ins),
            out_specs=(VMEM,) * len(outs),
            scratch_shapes=scratch,
            compiler_params=PARAMS,
            cost_estimate=cost(flops, 8_000_000),
            name=name,
        )(*ins)

    def core_swap(x):
        return lax.ppermute(x, "front", [(i, i ^ 1) for i in range(4)])

    def cross(x):
        def branch(mask):
            pairs = [(i, i ^ 2) for i in range(4) if mask >> i & 1]
            return lambda v: lax.ppermute(v, "front", pairs) if pairs else jnp.zeros_like(v)

        return lax.switch(crossing, [branch(mask) for mask in range(16)], x)

    x_groups = [[4 * y + x for x in range(4)] for y in range(8)]
    row_groups = [[8 * r + c for c in range(8)] for r in range(4)]
    z_groups = [[i, i + 16] for i in range(16)]
    low_half = col < 4

    def column_swap(x):
        return jnp.concatenate([x] + [swap(x, 8 * k) for k in range(1, 4)], 0)

    def x_swap(x):
        return [x] + [swap(x, k) for k in range(1, 4)]

    q0 = a[:BLK, :BLK]
    other = swap(q0, 4)
    rest = a[BLK:512, :256]
    other, rest = lax.optimization_barrier((other, rest))
    q0 = column_swap(jnp.where(low_half, q0, other))
    far = swap(rest, 4)
    q0, far = lax.optimization_barrier((q0, far))
    q0 = x_swap(q0)
    lo = jnp.where(low_half, rest, far)
    hi = jnp.where(low_half, far, rest)
    q12 = jnp.concatenate(
        [lo[:BLK, :BLK], hi[:BLK, :BLK], lo[BLK : 2 * BLK, :BLK], hi[BLK : 2 * BLK, :BLK], lo[BLK : 2 * BLK, BLK:]], 1
    )
    q12 = column_swap(q12)
    *q0, q12 = lax.optimization_barrier((*q0, q12))
    q1, q2 = x_swap(q12[:, : 2 * BLK]), q12[:, 2 * BLK :]
    q3 = jnp.concatenate([lo[2 * BLK :, :BLK], hi[2 * BLK :, :BLK], lo[2 * BLK :, BLK:], hi[2 * BLK :, BLK:]], 1)
    q3 = lax.all_gather(q3, "tile", axis=0, axis_index_groups=x_groups)
    side_top, side_low = a[:256, 256:], a[256:512, 256:]
    side_low = jnp.stack([side_low, swap(side_low, 8)])

    trail = a[512:, :256].reshape(2, 2, 384, 256)
    half = col // 4
    near = lax.dynamic_index_in_dim(trail, half, 1, keepdims=False)
    far = swap(lax.dynamic_index_in_dim(trail, 1 - half, 1, keepdims=False), 4)

    wa, top0 = call(kernel_a, "panel_a", 25_000_000_000, q0, (mid, top_shape), [quarter, block])
    wa, q2, q3, far, side_low, *q1 = lax.optimization_barrier((wa, q2, q3, far, side_low, *q1))
    side_top = lax.all_gather(side_top, "tile", axis=0, axis_index_groups=z_groups)
    q2 = x_swap(q2)
    q3_y, q3_z = swap(q3, 8), swap(q3, 16)
    w0hi, w0lo, top1 = call(
        kernel_b,
        "panel_b",
        32_000_000_000,
        q1 + [wa],
        (big, big, top_shape),
        [quarter, quarter, quarter, piece, piece, line, block],
    )
    w0hi, far, q3_y, side_top, *q2 = lax.optimization_barrier((w0hi, far, q3_y, side_top, *q2))
    q3 = [q3, q3_y, q3_z, swap(q3_y, 16)]
    both = jnp.concatenate([near, far], 2).reshape(2, 4, 96, 512)
    pieces = [
        lax.dynamic_index_in_dim(both, (col % 4) ^ k, 1, keepdims=False).reshape(192, 512) for k in range(4)
    ]
    pieces = pieces[:1] + [swap(pieces[k], k) for k in range(1, 4)]
    top_y = swap(side_top, 8)
    low_c, wc, top2 = call(
        kernel_c,
        "panel_c",
        35_000_000_000,
        q2 + [w0hi, w0lo],
        (wide, mid, top_shape),
        [quarter, strip, strip, pltpu.VMEM((BLK, 512), F32), block],
    )
    wc, top_y, *rest = lax.optimization_barrier((wc, top_y, *pieces, *q3))
    pieces, q3 = rest[:4], rest[4:]
    low_z = swap(side_low, 16)
    sub = jax.ShapeDtypeStruct((96, 1024), BF16)
    first = call(
        functools.partial(rows_kernel, 0),
        "first_rows",
        1_200_000_000,
        pieces + [w0hi, w0lo],
        (sub, sub),
        [pltpu.VMEM((192, 1024), F32)],
    )
    l0 = [lax.all_gather(x, "tile", axis=0, tiled=True, axis_index_groups=row_groups) for x in first]
    low_d, w1hi, w1lo, top3 = call(
        kernel_d,
        "panel_d",
        38_000_000_000,
        q3 + [w0hi, w0lo, low_c, wc],
        (wide, big, big, top_shape),
        [quarter, quarter, quarter, piece, piece, strip, strip, line, block],
    )
    w1hi, low_z = lax.optimization_barrier((w1hi, low_z))
    second = call(
        functools.partial(rows_kernel, 1),
        "second_rows",
        1_700_000_000,
        pieces + [w1hi, w1lo, low_c, low_d, *first],
        (sub, sub),
        [pltpu.VMEM((192, 1024), F32)],
    )
    l1 = [lax.all_gather(x, "tile", axis=0, tiled=True, axis_index_groups=row_groups) for x in second]
    w1lo, *l0 = lax.optimization_barrier((w1lo, *l0))
    tall = jax.ShapeDtypeStruct((1024, 768), BF16)
    t0, t1 = call(
        columns_kernel,
        "column_rows",
        12_000_000_000,
        [side_top, top_y, side_low, low_z, w0hi, w0lo, w1hi, w1lo, low_c, low_d],
        (tall, tall),
        [pltpu.VMEM((1024, 768), BF16)] * 2 + [pltpu.VMEM((1024, 768), F32)],
    )
    def update(h):
        def rows_of(k):
            return pl.BlockSpec((256, 256), lambda j: (2 + 3 * h + k, 1 + j))

        return pl.pallas_call(
            update_kernel,
            grid=(3,),
            out_shape=(
                jax.ShapeDtypeStruct((768, 768), BF16),
                jax.ShapeDtypeStruct((768, 256), BF16),
            ),
            in_specs=[
                pl.BlockSpec((768, 1024), lambda j: (0, 0)),
                pl.BlockSpec((768, 1024), lambda j: (0, 0)),
                pl.BlockSpec((1024, 256), lambda j: (0, j)),
                pl.BlockSpec((1024, 256), lambda j: (0, j)),
                rows_of(0),
                rows_of(1),
                rows_of(2),
            ],
            out_specs=(
                pl.BlockSpec((768, 256), lambda j: (0, j)),
                pl.BlockSpec((768, 256), lambda j: (0, 0)),
            ),
            compiler_params=PARAMS,
            cost_estimate=cost(2_500_000_000, 9_000_000),
            name="update",
        )(l0[h], l1[h], t0, t1, a, a, a)

    children, lower = [], []
    for h in range(2):
        if h:
            across, l1[1] = lax.optimization_barrier((across, l1[1]))
            children[0] = (*children[0][:2], across, core_swap(across))
        own, below = update(h)
        across = cross(own)
        children.append((own, core_swap(own), across, core_swap(across)))
        lower.append(below)
    factor = jnp.concatenate([top0, top1, top2, top3, *lower], 0)

    def child_spec(k, h):
        def index(i, rows, cols):
            at = rows[k, i] - 6 * h
            return jnp.where((at >= 0) & (at < 6), at, 0), 0

        return pl.BlockSpec((BLK, 768), index)

    order = [(k, h) for k in range(4) for h in range(2)]
    merged = pl.pallas_call(
        merge_kernel,
        grid_spec=pltpu.PrefetchScalarGridSpec(
            num_scalar_prefetch=2,
            grid=(16,),
            in_specs=[pl.BlockSpec((BLK, 1024), lambda i, rows, cols: (i, 0))] + [child_spec(k, h) for k, h in order],
            out_specs=pl.BlockSpec((BLK, 1024), lambda i, rows, cols: (i, 0)),
        ),
        out_shape=jax.ShapeDtypeStruct((2048, 1024), F32),
        compiler_params=PARAMS,
        cost_estimate=cost(10_000_000, 22_000_000),
        name="merge",
    )(from_rows, from_cols, parents[0, 0], *[children[h][k] for k, h in order])
    return factor[None, None], merged[None, None]


def solution(mesh):
    return jax.shard_map(
        per_device,
        mesh=mesh,
        in_specs=(P("front", "tile", None, None), P("front", "tile", None, None), P(), P()),
        out_specs=(P("front", "tile", None, None), P("front", "tile", None, None)),
        check_vma=False,
    )
```

```python
import functools

import jax
import jax.numpy as jnp
from jax import lax
from jax.experimental import pallas as pl
from jax.experimental.pallas import tpu as pltpu
from jax.sharding import PartitionSpec as P

BLK = 128
F32 = jnp.float32
BF16 = jnp.bfloat16
NN = (((1,), (0,)), ((), ()))
NT = (((1,), (1,)), ((), ()))


def dot(a, b, dims):
    return lax.dot_general(a, b, dims, preferred_element_type=F32)


def split(x):
    hi = x.astype(BF16)
    return hi, (x - hi.astype(F32)).astype(BF16)


def dot3(a, b, dims):
    return dot(a[0], b[0], dims) + (dot(a[0], b[1], dims) + dot(a[1], b[0], dims))


def dotp(a, b, dims):
    return dot3(split(a), split(b), dims)


def lane_of(x, lane):
    return jnp.broadcast_to(x[:, lane : lane + 1], (8, BLK))


def row_of(x, row):
    return jnp.broadcast_to(x[row : row + 1, :], (8, BLK))


def factor_block(rows, out_ref, out_row, out_col):
    S = list(rows)
    lanes = lax.broadcasted_iota(jnp.int32, (8, BLK), 1)
    subs = lax.broadcasted_iota(jnp.int32, (8, BLK), 0)
    G = [(lanes == subs + 8 * v).astype(F32) for v in range(16)]
    for v0 in range(16):
        C = {v: [lane_of(S[v], 8 * v0 + j) for j in range(8)] for v in range(v0, 16)}
        d = [[row_of(C[v0][j], i) if i >= j else None for j in range(8)] for i in range(8)]
        Rs = [row_of(S[v0], i) for i in range(8)]
        Rg = [row_of(G[v0], i) for i in range(8)]
        Cn = list(C[v0 + 1]) if v0 < 15 else None
        m = [[None] * 8 for _ in range(8)]
        Us, Ug = [None] * 8, [None] * 8
        wrows = None
        for j in range(8):
            rs = lax.rsqrt(d[j][j])
            p = rs * rs
            w = Rg[j] * rs
            wrows = w if j == 0 else jnp.where(subs == j, w, wrows)
            for i in range(j + 1, 8):
                m[i][j] = d[i][j] * p
            for i in range(j + 1, 8):
                for k in range(j + 1, i + 1):
                    d[i][k] = d[i][k] - m[i][j] * d[k][j]
            Us[j] = Rs[j] * p
            Ug[j] = Rg[j] * p
            if Cn is not None:
                S[v0 + 1] = S[v0 + 1] - Cn[j] * Us[j]
                G[v0 + 1] = G[v0 + 1] - Cn[j] * Ug[j]
            for i in range(j + 1, 8):
                Rs[i] = Rs[i] - m[i][j] * Rs[j]
                Rg[i] = Rg[i] - m[i][j] * Rg[j]
                if Cn is not None:
                    Cn[i] = Cn[i] - m[i][j] * Cn[j]
        out_ref[pl.ds(out_row + 8 * v0, 8), pl.ds(out_col, BLK)] = wrows
        if v0 < 14:
            for j in range(6, -1, -1):
                for i in range(j + 1, 8):
                    Us[j] = Us[j] - m[i][j] * Us[i]
                    Ug[j] = Ug[j] - m[i][j] * Ug[i]
            for v in range(v0 + 2, 16):
                for j in range(8):
                    S[v] = S[v] - C[v][j] * Us[j]
                    G[v] = G[v] - C[v][j] * Ug[j]


def chol_inverse(A, W, Ls):
    pairs = A.shape[0] // 256
    W[...] = jnp.zeros(W.shape, F32)

    def step(kb, _):
        r0 = pl.multiple_of(kb * BLK, BLK)
        rows = [A[pl.ds(pl.multiple_of(r0 + 8 * v, 8), 8), pl.ds(r0, BLK)] for v in range(16)]
        factor_block(rows, W, r0, r0)

        @pl.when(kb % 2 == 0)
        def _():
            r1 = pl.multiple_of(r0 + BLK, BLK)
            low = dot3(split(A[pl.ds(r1, BLK), pl.ds(r0, BLK)]), split(W[pl.ds(r0, BLK), pl.ds(r0, BLK)]), NT)
            Ls[...] = low
            low = split(low)
            A[pl.ds(r1, BLK), pl.ds(r1, BLK)] -= dot3(low, low, NT)

        @pl.when(kb % 2 == 1)
        def _():
            q = pl.multiple_of(r0 - BLK, BLK)
            t = dot3(split(Ls[...]), split(W[pl.ds(q, BLK), pl.ds(q, BLK)]), NN)
            W[pl.ds(r0, BLK), pl.ds(q, BLK)] = -dot3(split(W[pl.ds(r0, BLK), pl.ds(r0, BLK)]), split(t), NN)

        for c in range(pairs):
            @pl.when(kb == 2 * c + 1)
            def _():
                lo, hi = 256 * c, 256 * (c + 1)
                wd = split(W[lo:hi, lo:hi])
                if c > 0:
                    W[lo:hi, :lo] = dot3(wd, split(W[lo:hi, :lo]), NN)
                if c < pairs - 1:
                    low = split(dot3(split(A[hi:, lo:hi]), wd, NT))
                    for n in range(c + 1, pairs):
                        a, b = 256 * n, 256 * (n + 1)
                        A[a:, a:b] -= dot3([x[a - hi :] for x in low], [x[a - hi : b - hi] for x in low], NT)
                    W[hi:, lo:hi] = -dot3(low, wd, NN)
                    if c > 0:
                        W[hi:, :lo] -= dot3(low, split(W[lo:hi, :lo]), NN)

        return 0

    lax.fori_loop(0, 2 * pairs, step, 0)


VMEM = pl.BlockSpec(memory_space=pltpu.VMEM)
PARAMS = pltpu.CompilerParams(vmem_limit_bytes=56 * 2**20)


def cost(flops, data):
    return pl.CostEstimate(flops=flops, bytes_accessed=data, transcendentals=0)


def position():
    tile = lax.axis_index("tile")
    return tile // 8, tile % 8


def times_inverse_t(x, w, put):
    for n in range(4):
        a, b = 256 * n, 256 * (n + 1)
        put(n, dot3((x[0][:, :b], x[1][:, :b]), (w[0][a:b, :b], w[1][a:b, :b]), NT))


def inverse_times(w, x, put):
    for n in range(4):
        a, b = 256 * n, 256 * (n + 1)
        put(n, dot3((w[0][a:b, :b], w[1][a:b, :b]), (x[0][:b], x[1][:b]), NN))


def store_split(hi, lo, index, x):
    h, l = split(x)
    hi[index] = h
    lo[index] = l


def block_at(index):
    return pl.ds(pl.multiple_of(index * BLK, BLK), BLK)


def finish_lower(whi, wlo, wa, low, wb):
    first, last = split(wa[...]), split(wb[...])
    below = split(-dot3(last, split(dot3(low, first, NN)), NN))
    for out, d0, d1, x in zip((whi, wlo), first, last, below):
        out[:512, :512] = d0
        out[:512, 512:] = jnp.zeros((512, 512), BF16)
        out[512:, :512] = x
        out[512:, 512:] = d1


def own_part(left, whi, wlo, index):
    return dot3(split(left), (whi[block_at(index), :], wlo[block_at(index), :]), NT)


def kernel_a(*refs):
    pieces = refs[:4]
    wa, top, A, Ls = refs[4:]
    row, col = position()
    here = (row + 3) % 4
    for k in range(4):
        for n in range(4):
            A[block_at(((row ^ n) + 3) % 4), block_at((col % 4) ^ k)] = pieces[k][n * BLK : (n + 1) * BLK, :]
    keep = A[block_at(here), :]
    chol_inverse(A, wa, Ls)
    own = dotp(keep, wa[block_at(col % 4), :], NT)
    top[:, :BLK] = jnp.where((col < 4) & (here >= col), own, 0.0).astype(BF16)
    top[:, BLK:] = jnp.zeros((BLK, BLK), BF16)


def kernel_b(*refs):
    pieces = refs[:4]
    wa, whi, wlo, top, D, A, wb, lhi, llo, keep, Ls = refs[4:]
    row, col = position()
    here = (row + 3) % 4
    for k in range(4):
        for n in range(4):
            at = block_at(((row ^ n) + 3) % 4), block_at((col % 4) ^ k)
            D[at] = pieces[k][n * BLK : (n + 1) * BLK, :BLK]
            A[at] = pieces[k][n * BLK : (n + 1) * BLK, BLK:]
    keep[:, :512] = D[block_at(here), :]
    keep[:, 512:] = A[block_at(here), :]
    low = split(dot3(split(D[...]), split(wa[...]), NT))
    lhi[...], llo[...] = low
    A[...] -= dot3(low, low, NT)
    chol_inverse(A, wb, Ls)
    finish_lower(whi, wlo, wa, (lhi[...], llo[...]), wb)
    own = own_part(keep[...], whi, wlo, col)
    top[:, :BLK] = jnp.where(here + 4 >= col, own, 0.0).astype(BF16)
    top[:, BLK:] = jnp.zeros((BLK, BLK), BF16)


def place(src, i, x, xhi, xlo, blocks):
    rows = block_at(i)
    for half in range(2):
        store_split(xhi, xlo, (rows, block_at(4 * half + x)), src[:, half * BLK : (half + 1) * BLK])
    for n, ref in enumerate(blocks):
        ref[rows, block_at(x)] = src[:, (n + 2) * BLK : (n + 3) * BLK]


def spread(pieces, row, xhi, xlo, blocks):
    for k in range(4):
        for x in range(4):
            place(pieces[k][x], ((row ^ k) + 3) % 4, x, xhi, xlo, blocks)


def kernel_c(*refs):
    pieces = refs[:4]
    w0hi, w0lo, low, wc, top, A, xhi, xlo, keep, Ls = refs[4:]
    row, col = position()
    here = (row + 3) % 4
    for k in range(4):
        for n in range(4):
            place(pieces[k][n * BLK : (n + 1) * BLK, :], ((row ^ n) + 3) % 4, (col % 4) ^ k, xhi, xlo, [A])

    def put(n, x):
        low[:, 256 * n : 256 * (n + 1)] = x.astype(BF16)

    times_inverse_t((xhi, xlo), (w0hi, w0lo), put)
    A[...] -= dot(low[...], low[...], NT)
    keep[...] = A[block_at(here), :]
    chol_inverse(A, wc, Ls)
    own = dotp(keep[...], wc[block_at(col % 4), :], NT)
    top[:, :BLK] = low[block_at(here), block_at(col)]
    top[:, BLK:] = jnp.where((col < 4) & (here >= col), own, 0.0).astype(BF16)


def kernel_d(*refs):
    pieces = refs[:4]
    w0hi, w0lo, lowc, wc, low, whi, wlo, top, D, A, wd, lhi, llo, xhi, xlo, keep, Ls = refs[4:]
    row, col = position()
    here = (row + 3) % 4
    spread(pieces, row, xhi, xlo, [D, A])

    def put(n, x):
        low[:, 256 * n : 256 * (n + 1)] = x.astype(BF16)

    times_inverse_t((xhi, xlo), (w0hi, w0lo), put)
    D[...] -= dot(low[...], lowc[...], NT)
    A[...] -= dot(low[...], low[...], NT)
    keep[:, :512] = D[block_at(here), :]
    keep[:, 512:] = A[block_at(here), :]
    lower = split(dot3(split(D[...]), split(wc[...]), NT))
    lhi[...], llo[...] = lower
    A[...] -= dot3(lower, lower, NT)
    chol_inverse(A, wd, Ls)
    finish_lower(whi, wlo, wc, (lhi[...], llo[...]), wd)
    own = own_part(keep[...], whi, wlo, col)
    top[:, :BLK] = low[block_at(here), block_at(col)]
    top[:, BLK:] = jnp.where(here + 4 >= col, own, 0.0).astype(BF16)


def rows_kernel(panel, *refs):
    pieces, refs = refs[:4], refs[4:]
    row, col = position()
    if panel == 0:
        whi, wlo, out, x = refs
    else:
        whi, wlo, low_c, low_d, first, out, x = refs
    for k in range(4):
        for n in range(2):
            at = (2 * n + panel) * BLK
            x[:, block_at(col ^ k ^ (4 * n))] = pieces[k][:, at : at + BLK]
    v = x[...]
    if panel == 1:
        v = v - jnp.concatenate([dot(first[...].reshape(192, 1024), low[...], NT) for low in (low_c, low_d)], 1)

    def put(n, y):
        for h in range(2):
            out[h, :, 256 * n : 256 * (n + 1)] = y[96 * h : 96 * (h + 1)].astype(BF16)

    times_inverse_t(split(v), (whi, wlo), put)


def columns_kernel(top_z, top_y, low_own, low_z, w0hi, w0lo, w1hi, w1lo, low_c, low_d, t0, t1, xhi, xlo, y):
    row, _ = position()
    for n in range(2):
        for top, side in ((top_z, row % 2), (top_y, 1 - row % 2)):
            at = (2 * n + side + 3) % 4
            for m in range(2):
                store_split(xhi, xlo, (block_at(4 * m + at), slice(None)), top[n, m * BLK : (m + 1) * BLK, :])
        for low, flip in ((low_own, n), (low_z, n + 2)):
            at = ((row ^ flip) + 3) % 4
            for m in range(2):
                y[block_at(4 * m + at), :] = low[n, m * BLK : (m + 1) * BLK, :]

    def put(t):
        def go(n, v):
            t[256 * n : 256 * (n + 1), :] = v.astype(BF16)

        return go

    inverse_times((w0hi, w0lo), (xhi, xlo), put(t0))
    for n in range(4):
        at = slice(256 * n, 256 * (n + 1)), slice(None)
        low = (low_c, low_d)[n // 2]
        part = slice(256 * (n % 2), 256 * (n % 2 + 1))
        store_split(xhi, xlo, at, y[at] - dot(low[part, :], t0[...], NN))
    inverse_times((w1hi, w1lo), (xhi, xlo), put(t1))


def update_kernel(l0, *refs):
    pieces, (t0, t1, a0, a1, a2, out, factor, l1) = refs[:4], refs[4:]
    _, col = position()

    @pl.when(pl.program_id(0) == 0)
    def _():
        for k in range(4):
            for n in range(2):
                l1[pl.ds(pl.multiple_of((col ^ k ^ (4 * n)) * 96, 32), 96), :] = pieces[k][n]
        at = block_at(col)
        factor[:, :BLK] = l0[:, 0, :, at].reshape(768, BLK)
        factor[:, BLK:] = l1[:, at]

    total = dot(l0[:, 0].reshape(768, 1024), t0[...], NN) + dot(l1[...], t1[...], NN)
    for n, a in enumerate((a0, a1, a2)):
        at = slice(256 * n, 256 * (n + 1))
        out[at, :] = (a[...] - total[at]).astype(BF16)


def merge_kernel(rows, cols, parent, *refs):
    children, (out, held, sem) = refs[:8], refs[8:]
    step = pl.program_id(0)

    def copies(k):
        return [
            pltpu.make_async_copy(children[2 * k + h], held.at[k, pl.ds(768 * h, 768), :], sem.at[k, h])
            for h in range(2)
        ]

    for k in range(4):
        @pl.when((step == 0) & (cols[k, 8] > 0))
        def _():
            for copy in copies(k):
                copy.start()

    out[...] = parent[...].astype(F32)

    for k in range(4):
        @pl.when((step == 0) & (cols[k, 8] > 0))
        def _():
            for copy in copies(k):
                copy.wait()

    for k in range(4):
        for i in range(2):
            a = rows[k, 2 * step + i]

            @pl.when(a >= 0)
            def _():
                for j in range(8):
                    b = cols[k, j]
                    x = held[k, block_at(a), block_at(jnp.maximum(b, 0))].astype(F32)
                    out[i * BLK : (i + 1) * BLK, j * BLK : (j + 1) * BLK] += jnp.where(b >= 0, x, 0.0)


def per_device(fronts, parents, parent_of, block_map):
    tile = lax.axis_index("tile")
    row, col = tile // 8, tile % 8
    my_front = lax.axis_index("front")
    a = fronts[0, 0]
    big = jax.ShapeDtypeStruct((1024, 1024), BF16)
    mid = jax.ShapeDtypeStruct((512, 512), F32)
    wide = jax.ShapeDtypeStruct((512, 1024), BF16)
    top_shape = jax.ShapeDtypeStruct((BLK, 256), BF16)
    piece = pltpu.VMEM((512, 512), BF16)
    quarter = pltpu.VMEM((512, 512), F32)
    strip = pltpu.VMEM((512, 1024), BF16)
    line = pltpu.VMEM((BLK, 1024), F32)
    block = pltpu.VMEM((BLK, BLK), F32)

    place_r = jnp.arange(12) * 4 + (row + 3) % 4
    place_c = jnp.arange(6) * 8 + col
    child = my_front ^ jnp.arange(4)
    child_map = block_map[child]
    at_rows = child_map[:, place_r] // 4
    at_cols = child_map[:, place_c] // 8
    mine = (parent_of[child] == my_front)[:, None]
    crossing = jnp.sum(jnp.where(parent_of // 2 != jnp.arange(4) // 2, 1 << jnp.arange(4), 0))
    hit_r = (at_rows[:, :, None] == jnp.arange(16)) & mine[:, :, None]
    hit_c = at_cols[:, :, None] == jnp.arange(8)
    from_rows = jnp.max(jnp.where(hit_r, jnp.arange(12)[:, None], -1), axis=1).astype(jnp.int32)
    from_cols = jnp.max(jnp.where(hit_c, jnp.arange(6)[:, None], -1), axis=1).astype(jnp.int32)
    from_cols = jnp.concatenate([from_cols, mine.astype(jnp.int32)], 1)

    def swap(x, k):
        return lax.ppermute(x, "tile", [(i, i ^ k) for i in range(32)])

    def call(kernel, name, flops, ins, outs, scratch):
        return pl.pallas_call(
            kernel,
            out_shape=outs,
            in_specs=[VMEM] * len(ins),
            out_specs=(VMEM,) * len(outs),
            scratch_shapes=scratch,
            compiler_params=PARAMS,
            cost_estimate=cost(flops, 8_000_000),
            name=name,
        )(*ins)

    def core_swap(x):
        return lax.ppermute(x, "front", [(i, i ^ 1) for i in range(4)])

    def cross(x):
        def branch(mask):
            pairs = [(i, i ^ 2) for i in range(4) if mask >> i & 1]
            return lambda v: lax.ppermute(v, "front", pairs) if pairs else jnp.zeros_like(v)

        return lax.switch(crossing, [branch(mask) for mask in range(16)], x)

    x_groups = [[4 * y + x for x in range(4)] for y in range(8)]
    row_groups = [[8 * r + c for c in range(8)] for r in range(4)]
    z_groups = [[i, i + 16] for i in range(16)]
    low_half = col < 4

    def column_swap(x):
        return jnp.concatenate([x] + [swap(x, 8 * k) for k in range(1, 4)], 0)

    def x_swap(x):
        return [x] + [swap(x, k) for k in range(1, 4)]

    q0 = a[:BLK, :BLK]
    other = swap(q0, 4)
    rest = a[BLK:512, :256]
    other, rest = lax.optimization_barrier((other, rest))
    q0 = column_swap(jnp.where(low_half, q0, other))
    far = swap(rest, 4)
    q0, far = lax.optimization_barrier((q0, far))
    q0 = x_swap(q0)
    lo = jnp.where(low_half, rest, far)
    hi = jnp.where(low_half, far, rest)
    q12 = jnp.concatenate(
        [lo[:BLK, :BLK], hi[:BLK, :BLK], lo[BLK : 2 * BLK, :BLK], hi[BLK : 2 * BLK, :BLK], lo[BLK : 2 * BLK, BLK:]], 1
    )
    q12 = column_swap(q12)
    *q0, q12, lo, hi = lax.optimization_barrier((*q0, q12, lo, hi))
    q1, q2 = x_swap(q12[:, : 2 * BLK]), q12[:, 2 * BLK :]
    q3 = jnp.concatenate([lo[2 * BLK :, :BLK], hi[2 * BLK :, :BLK], lo[2 * BLK :, BLK:], hi[2 * BLK :, BLK:]], 1)
    q3 = lax.all_gather(q3, "tile", axis=0, axis_index_groups=x_groups)
    side_top, side_low = a[:256, 256:], a[256:512, 256:]
    side_low = jnp.stack([side_low, swap(side_low, 8)])

    trail = a[512:, :256].reshape(2, 2, 384, 256)
    half = col // 4
    near = lax.dynamic_index_in_dim(trail, half, 1, keepdims=False)
    far = swap(lax.dynamic_index_in_dim(trail, 1 - half, 1, keepdims=False), 4)

    wa, top0 = call(kernel_a, "panel_a", 25_000_000_000, q0, (mid, top_shape), [quarter, block])
    wa, q2, q3, far, side_low, *q1 = lax.optimization_barrier((wa, q2, q3, far, side_low, *q1))
    side_top = lax.all_gather(side_top, "tile", axis=0, axis_index_groups=z_groups)
    q2 = x_swap(q2)
    q3_y, q3_z = swap(q3, 8), swap(q3, 16)
    w0hi, w0lo, top1 = call(
        kernel_b,
        "panel_b",
        32_000_000_000,
        q1 + [wa],
        (big, big, top_shape),
        [quarter, quarter, quarter, piece, piece, line, block],
    )
    w0hi, far, q3_y, side_top, *q2 = lax.optimization_barrier((w0hi, far, q3_y, side_top, *q2))
    q3 = [q3, q3_y, q3_z, swap(q3_y, 16)]
    both = jnp.concatenate([near, far], 2).reshape(2, 4, 96, 512)
    pieces = [
        lax.dynamic_index_in_dim(both, (col % 4) ^ k, 1, keepdims=False).reshape(192, 512) for k in range(4)
    ]
    pieces = pieces[:1] + [swap(pieces[k], k) for k in range(1, 4)]
    top_y = swap(side_top, 8)
    low_c, wc, top2 = call(
        kernel_c,
        "panel_c",
        35_000_000_000,
        q2 + [w0hi, w0lo],
        (wide, mid, top_shape),
        [quarter, strip, strip, pltpu.VMEM((BLK, 512), F32), block],
    )
    wc, top_y, *rest = lax.optimization_barrier((wc, top_y, *pieces, *q3))
    pieces, q3 = rest[:4], rest[4:]
    low_z = swap(side_low, 16)
    sub = jax.ShapeDtypeStruct((2, 96, 1024), BF16)
    (first,) = call(
        functools.partial(rows_kernel, 0),
        "first_rows",
        1_200_000_000,
        pieces + [w0hi, w0lo],
        (sub,),
        [pltpu.VMEM((192, 1024), F32)],
    )
    l0 = lax.all_gather(first, "tile", axis=0, axis_index_groups=row_groups)
    low_d, w1hi, w1lo, top3 = call(
        kernel_d,
        "panel_d",
        38_000_000_000,
        q3 + [w0hi, w0lo, low_c, wc],
        (wide, big, big, top_shape),
        [quarter, quarter, quarter, piece, piece, strip, strip, line, block],
    )
    w1hi, low_z = lax.optimization_barrier((w1hi, low_z))
    (second,) = call(
        functools.partial(rows_kernel, 1),
        "second_rows",
        1_700_000_000,
        pieces + [w1hi, w1lo, low_c, low_d, first],
        (sub,),
        [pltpu.VMEM((192, 1024), F32)],
    )
    pair = swap(second, 4)
    later = jnp.stack([second[1], pair[1]])
    l1 = x_swap(jnp.stack([second[0], pair[0]]))
    tall = jax.ShapeDtypeStruct((1024, 768), BF16)
    t0, t1 = call(
        columns_kernel,
        "column_rows",
        12_000_000_000,
        [side_top, top_y, side_low, low_z, w0hi, w0lo, w1hi, w1lo, low_c, low_d],
        (tall, tall),
        [pltpu.VMEM((1024, 768), BF16)] * 2 + [pltpu.VMEM((1024, 768), F32)],
    )
    t0, later = lax.optimization_barrier((t0, later))
    l1 = [l1, x_swap(later)]

    def update(h):
        def rows_of(k):
            return pl.BlockSpec((256, 256), lambda j: (2 + 3 * h + k, 1 + j))

        return pl.pallas_call(
            update_kernel,
            grid=(3,),
            out_shape=(
                jax.ShapeDtypeStruct((768, 768), BF16),
                jax.ShapeDtypeStruct((768, 256), BF16),
            ),
            in_specs=[
                pl.BlockSpec((8, 1, 96, 1024), lambda j: (0, h, 0, 0)),
                *[pl.BlockSpec((2, 96, 1024), lambda j: (0, 0, 0))] * 4,
                pl.BlockSpec((1024, 256), lambda j: (0, j)),
                pl.BlockSpec((1024, 256), lambda j: (0, j)),
                rows_of(0),
                rows_of(1),
                rows_of(2),
            ],
            out_specs=(
                pl.BlockSpec((768, 256), lambda j: (0, j)),
                pl.BlockSpec((768, 256), lambda j: (0, 0)),
            ),
            scratch_shapes=[pltpu.VMEM((768, 1024), BF16)],
            compiler_params=PARAMS,
            cost_estimate=cost(2_500_000_000, 9_000_000),
            name="update",
        )(l0, *l1[h], t0, t1, a, a, a)

    children, lower = [], []
    for h in range(2):
        if h:
            across, *l1[1] = lax.optimization_barrier((across, *l1[1]))
            children[0] = (*children[0][:2], across, core_swap(across))
        own, below = update(h)
        across = cross(own)
        children.append((own, core_swap(own), across, core_swap(across)))
        lower.append(below)
    factor = jnp.concatenate([top0, top1, top2, top3, *lower], 0)

    merged = pl.pallas_call(
        merge_kernel,
        grid_spec=pltpu.PrefetchScalarGridSpec(
            num_scalar_prefetch=2,
            grid=(8,),
            in_specs=[pl.BlockSpec((2 * BLK, 1024), lambda i, rows, cols: (i, 0))]
            + [pl.BlockSpec(memory_space=pl.ANY)] * 8,
            out_specs=pl.BlockSpec((2 * BLK, 1024), lambda i, rows, cols: (i, 0)),
            scratch_shapes=[pltpu.VMEM((4, 1536, 768), BF16), pltpu.SemaphoreType.DMA((4, 2))],
        ),
        out_shape=jax.ShapeDtypeStruct((2048, 1024), F32),
        compiler_params=PARAMS,
        cost_estimate=cost(10_000_000, 22_000_000),
        name="merge",
    )(from_rows, from_cols, parents[0, 0], *[children[h][k] for k in range(4) for h in range(2)])
    return factor[None, None], merged[None, None]


def solution(mesh):
    return jax.shard_map(
        per_device,
        mesh=mesh,
        in_specs=(P("front", "tile", None, None), P("front", "tile", None, None), P(), P()),
        out_specs=(P("front", "tile", None, None), P("front", "tile", None, None)),
        check_vma=False,
    )
```

```python
import functools

import jax
import jax.numpy as jnp
from jax import lax
from jax.experimental import pallas as pl
from jax.experimental.pallas import tpu as pltpu
from jax.sharding import PartitionSpec as P

BLK = 128
F32 = jnp.float32
BF16 = jnp.bfloat16
NN = (((1,), (0,)), ((), ()))
NT = (((1,), (1,)), ((), ()))


def dot(a, b, dims):
    return lax.dot_general(a, b, dims, preferred_element_type=F32)


def split(x):
    hi = x.astype(BF16)
    return hi, (x - hi.astype(F32)).astype(BF16)


def dot3(a, b, dims):
    return dot(a[0], b[0], dims) + (dot(a[0], b[1], dims) + dot(a[1], b[0], dims))


def dotp(a, b, dims):
    return dot3(split(a), split(b), dims)


def lane_of(x, lane):
    return jnp.broadcast_to(x[:, lane : lane + 1], (8, BLK))


def factor_block(rows, out_ref, out_row, out_col, T):
    S = list(rows)
    lanes = lax.broadcasted_iota(jnp.int32, (8, BLK), 1)
    subs = lax.broadcasted_iota(jnp.int32, (8, BLK), 0)
    G = [(lanes == subs + 8 * v).astype(F32) for v in range(16)]
    for v0 in range(16):
        C = {v: [lane_of(S[v], 8 * v0 + j) for j in range(8)] for v in range(v0, 16)}
        at = 80 * (v0 % 2)
        for n, x in enumerate([*C[v0], S[v0], G[v0]]):
            T[at + 8 * n : at + 8 * n + 8, :] = x

        def spread_row(n, i):
            return T[pl.ds(at + 8 * n + i, 8, stride=0), :]

        d = [[spread_row(j, i) if i >= j else None for j in range(8)] for i in range(8)]
        Rs = [spread_row(8, i) for i in range(8)]
        Rg = [spread_row(9, i) for i in range(8)]
        Cn = list(C[v0 + 1]) if v0 < 15 else None
        m = [[None] * 8 for _ in range(8)]
        Us, Ug = [None] * 8, [None] * 8
        wrows = None
        for j in range(8):
            rs = lax.rsqrt(d[j][j])
            p = rs * rs
            w = Rg[j] * rs
            wrows = w if j == 0 else jnp.where(subs == j, w, wrows)
            for i in range(j + 1, 8):
                m[i][j] = d[i][j] * p
            for i in range(j + 1, 8):
                for k in range(j + 1, i + 1):
                    d[i][k] = d[i][k] - m[i][j] * d[k][j]
            Us[j] = Rs[j] * p
            Ug[j] = Rg[j] * p
            if Cn is not None:
                S[v0 + 1] = S[v0 + 1] - Cn[j] * Us[j]
                G[v0 + 1] = G[v0 + 1] - Cn[j] * Ug[j]
            for i in range(j + 1, 8):
                Rs[i] = Rs[i] - m[i][j] * Rs[j]
                Rg[i] = Rg[i] - m[i][j] * Rg[j]
                if Cn is not None:
                    Cn[i] = Cn[i] - m[i][j] * Cn[j]
        out_ref[pl.ds(out_row + 8 * v0, 8), pl.ds(out_col, BLK)] = wrows
        if v0 < 14:
            for j in range(6, -1, -1):
                for i in range(j + 1, 8):
                    Us[j] = Us[j] - m[i][j] * Us[i]
                    Ug[j] = Ug[j] - m[i][j] * Ug[i]
            for v in range(v0 + 2, 16):
                for j in range(8):
                    S[v] = S[v] - C[v][j] * Us[j]
                    G[v] = G[v] - C[v][j] * Ug[j]


def chol_inverse(A, W, Ls, T):
    pairs = A.shape[0] // 256
    W[...] = jnp.zeros(W.shape, F32)

    def step(kb, _):
        r0 = pl.multiple_of(kb * BLK, BLK)
        rows = [A[pl.ds(pl.multiple_of(r0 + 8 * v, 8), 8), pl.ds(r0, BLK)] for v in range(16)]
        factor_block(rows, W, r0, r0, T)

        @pl.when(kb % 2 == 0)
        def _():
            r1 = pl.multiple_of(r0 + BLK, BLK)
            low = dot3(split(A[pl.ds(r1, BLK), pl.ds(r0, BLK)]), split(W[pl.ds(r0, BLK), pl.ds(r0, BLK)]), NT)
            Ls[...] = low
            low = split(low)
            A[pl.ds(r1, BLK), pl.ds(r1, BLK)] -= dot3(low, low, NT)

        @pl.when(kb % 2 == 1)
        def _():
            q = pl.multiple_of(r0 - BLK, BLK)
            t = dot3(split(Ls[...]), split(W[pl.ds(q, BLK), pl.ds(q, BLK)]), NN)
            W[pl.ds(r0, BLK), pl.ds(q, BLK)] = -dot3(split(W[pl.ds(r0, BLK), pl.ds(r0, BLK)]), split(t), NN)

        for c in range(pairs):
            @pl.when(kb == 2 * c + 1)
            def _():
                lo, hi = 256 * c, 256 * (c + 1)
                wd = split(W[lo:hi, lo:hi])
                if c > 0:
                    W[lo:hi, :lo] = dot3(wd, split(W[lo:hi, :lo]), NN)
                if c < pairs - 1:
                    low = split(dot3(split(A[hi:, lo:hi]), wd, NT))
                    for n in range(c + 1, pairs):
                        a, b = 256 * n, 256 * (n + 1)
                        A[a:, a:b] -= dot3([x[a - hi :] for x in low], [x[a - hi : b - hi] for x in low], NT)
                    W[hi:, lo:hi] = -dot3(low, wd, NN)
                    if c > 0:
                        W[hi:, :lo] -= dot3(low, split(W[lo:hi, :lo]), NN)

        return 0

    lax.fori_loop(0, 2 * pairs, step, 0)


VMEM = pl.BlockSpec(memory_space=pltpu.VMEM)
PARAMS = pltpu.CompilerParams(vmem_limit_bytes=56 * 2**20)


def cost(flops, data):
    return pl.CostEstimate(flops=flops, bytes_accessed=data, transcendentals=0)


def position():
    tile = lax.axis_index("tile")
    return tile // 8, tile % 8


def times_inverse_t(x, w, put):
    for n in range(4):
        a, b = 256 * n, 256 * (n + 1)
        put(n, dot3((x[0][:, :b], x[1][:, :b]), (w[0][a:b, :b], w[1][a:b, :b]), NT))


def inverse_times(w, x, put):
    for n in range(4):
        a, b = 256 * n, 256 * (n + 1)
        put(n, dot3((w[0][a:b, :b], w[1][a:b, :b]), (x[0][:b], x[1][:b]), NN))


def store_split(hi, lo, index, x):
    h, l = split(x)
    hi[index] = h
    lo[index] = l


def block_at(index):
    return pl.ds(pl.multiple_of(index * BLK, BLK), BLK)


def finish_lower(whi, wlo, wa, low, wb):
    first, last = split(wa[...]), split(wb[...])
    below = split(-dot3(last, split(dot3(low, first, NN)), NN))
    for out, d0, d1, x in zip((whi, wlo), first, last, below):
        out[:512, :512] = d0
        out[:512, 512:] = jnp.zeros((512, 512), BF16)
        out[512:, :512] = x
        out[512:, 512:] = d1


def own_part(left, whi, wlo, index):
    return dot3(split(left), (whi[block_at(index), :], wlo[block_at(index), :]), NT)


def kernel_a(*refs):
    pieces = refs[:4]
    wa, top, A, Ls, T = refs[4:]
    row, col = position()
    here = (row + 3) % 4
    for k in range(4):
        for n in range(4):
            A[block_at(((row ^ n) + 3) % 4), block_at((col % 4) ^ k)] = pieces[k][n * BLK : (n + 1) * BLK, :]
    keep = A[block_at(here), :]
    chol_inverse(A, wa, Ls, T)
    own = dotp(keep, wa[block_at(col % 4), :], NT)
    top[:, :BLK] = jnp.where((col < 4) & (here >= col), own, 0.0).astype(BF16)
    top[:, BLK:] = jnp.zeros((BLK, BLK), BF16)


def kernel_b(*refs):
    pieces = refs[:4]
    wa, whi, wlo, top, D, A, wb, lhi, llo, keep, Ls, T = refs[4:]
    row, col = position()
    here = (row + 3) % 4
    for k in range(4):
        for n in range(4):
            at = block_at(((row ^ n) + 3) % 4), block_at((col % 4) ^ k)
            D[at] = pieces[k][n * BLK : (n + 1) * BLK, :BLK]
            A[at] = pieces[k][n * BLK : (n + 1) * BLK, BLK:]
    keep[:, :512] = D[block_at(here), :]
    keep[:, 512:] = A[block_at(here), :]
    low = split(dot3(split(D[...]), split(wa[...]), NT))
    lhi[...], llo[...] = low
    A[...] -= dot3(low, low, NT)
    chol_inverse(A, wb, Ls, T)
    finish_lower(whi, wlo, wa, (lhi[...], llo[...]), wb)
    own = own_part(keep[...], whi, wlo, col)
    top[:, :BLK] = jnp.where(here + 4 >= col, own, 0.0).astype(BF16)
    top[:, BLK:] = jnp.zeros((BLK, BLK), BF16)


def place(src, i, x, xhi, xlo, blocks):
    rows = block_at(i)
    for half in range(2):
        store_split(xhi, xlo, (rows, block_at(4 * half + x)), src[:, half * BLK : (half + 1) * BLK])
    for n, ref in enumerate(blocks):
        ref[rows, block_at(x)] = src[:, (n + 2) * BLK : (n + 3) * BLK]


def spread(pieces, row, xhi, xlo, blocks):
    for k in range(4):
        for x in range(4):
            place(pieces[k][x], ((row ^ k) + 3) % 4, x, xhi, xlo, blocks)


def kernel_c(*refs):
    pieces = refs[:4]
    w0hi, w0lo, low, wc, top, A, xhi, xlo, keep, Ls, T = refs[4:]
    row, col = position()
    here = (row + 3) % 4
    for k in range(4):
        for n in range(4):
            place(pieces[k][n * BLK : (n + 1) * BLK, :], ((row ^ n) + 3) % 4, (col % 4) ^ k, xhi, xlo, [A])

    def put(n, x):
        low[:, 256 * n : 256 * (n + 1)] = x.astype(BF16)

    times_inverse_t((xhi, xlo), (w0hi, w0lo), put)
    A[...] -= dot(low[...], low[...], NT)
    keep[...] = A[block_at(here), :]
    chol_inverse(A, wc, Ls, T)
    own = dotp(keep[...], wc[block_at(col % 4), :], NT)
    top[:, :BLK] = low[block_at(here), block_at(col)]
    top[:, BLK:] = jnp.where((col < 4) & (here >= col), own, 0.0).astype(BF16)


def kernel_d(*refs):
    pieces = refs[:4]
    w0hi, w0lo, lowc, wc, low, whi, wlo, top, D, A, wd, lhi, llo, xhi, xlo, keep, Ls, T = refs[4:]
    row, col = position()
    here = (row + 3) % 4
    spread(pieces, row, xhi, xlo, [D, A])

    def put(n, x):
        low[:, 256 * n : 256 * (n + 1)] = x.astype(BF16)

    times_inverse_t((xhi, xlo), (w0hi, w0lo), put)
    D[...] -= dot(low[...], lowc[...], NT)
    A[...] -= dot(low[...], low[...], NT)
    keep[:, :512] = D[block_at(here), :]
    keep[:, 512:] = A[block_at(here), :]
    lower = split(dot3(split(D[...]), split(wc[...]), NT))
    lhi[...], llo[...] = lower
    A[...] -= dot3(lower, lower, NT)
    chol_inverse(A, wd, Ls, T)
    finish_lower(whi, wlo, wc, (lhi[...], llo[...]), wd)
    own = own_part(keep[...], whi, wlo, col)
    top[:, :BLK] = low[block_at(here), block_at(col)]
    top[:, BLK:] = jnp.where(here + 4 >= col, own, 0.0).astype(BF16)


def rows_kernel(panel, *refs):
    pieces, refs = refs[:4], refs[4:]
    row, col = position()
    if panel == 0:
        whi, wlo, out, x = refs
    else:
        whi, wlo, low_c, low_d, first, out, x = refs
    for k in range(4):
        for n in range(2):
            at = (2 * n + panel) * BLK
            x[:, block_at(col ^ k ^ (4 * n))] = pieces[k][:, at : at + BLK]
    v = x[...]
    if panel == 1:
        v = v - jnp.concatenate([dot(first[...].reshape(192, 1024), low[...], NT) for low in (low_c, low_d)], 1)

    def put(n, y):
        for h in range(2):
            out[h, :, 256 * n : 256 * (n + 1)] = y[96 * h : 96 * (h + 1)].astype(BF16)

    times_inverse_t(split(v), (whi, wlo), put)


def columns_first(*refs):
    top_z, top_y = refs[:2]
    lows = refs[2:6]
    w0hi, w0lo, low_c, low_d, t0, nhi, nlo, xhi, xlo, y = refs[6:]
    row, _ = position()
    for n in range(2):
        for top, side in ((top_z, row % 2), (top_y, 1 - row % 2)):
            at = (2 * n + side + 3) % 4
            for m in range(2):
                store_split(xhi, xlo, (block_at(4 * m + at), slice(None)), top[n, m * BLK : (m + 1) * BLK, :])
    for k in range(4):
        at = ((row ^ k) + 3) % 4
        for m in range(2):
            y[block_at(4 * m + at), :] = lows[k][m * BLK : (m + 1) * BLK, :]

    def put(n, v):
        t0[256 * n : 256 * (n + 1), :] = v.astype(BF16)

    inverse_times((w0hi, w0lo), (xhi, xlo), put)
    for n in range(2):
        at = slice(512 * n, 512 * (n + 1)), slice(None)
        store_split(nhi, nlo, at, y[at] - dot((low_c, low_d)[n][...], t0[...], NN))


def columns_second(nhi, nlo, whi, wlo, t1):
    def put(n, v):
        t1[256 * n : 256 * (n + 1), :] = v.astype(BF16)

    inverse_times((whi, wlo), (nhi, nlo), put)


def update_kernel(l0, *refs):
    pieces, (t0, t1, a0, a1, a2, out, factor, l1) = refs[:4], refs[4:]
    _, col = position()

    @pl.when(pl.program_id(0) == 0)
    def _():
        for k in range(4):
            for n in range(2):
                l1[pl.ds(pl.multiple_of((col ^ k ^ (4 * n)) * 96, 32), 96), :] = pieces[k][n]
        at = block_at(col)
        factor[:, :BLK] = l0[:, 0, :, at].reshape(768, BLK)
        factor[:, BLK:] = l1[:, at]

    total = dot(l0[:, 0].reshape(768, 1024), t0[...], NN) + dot(l1[...], t1[...], NN)
    for n, a in enumerate((a0, a1, a2)):
        at = slice(256 * n, 256 * (n + 1))
        out[at, :] = (a[...] - total[at]).astype(BF16)


def merge_kernel(owner, block_map, parent, *refs):
    children, (out, held, sem) = refs[:8], refs[8:]
    step = pl.program_id(0)
    me = lax.axis_index("front")
    row, col = position()
    here = (row + 3) % 4

    def copies(k):
        return [
            pltpu.make_async_copy(children[2 * k + h], held.at[k, pl.ds(768 * h, 768), :], sem.at[k, h])
            for h in range(2)
        ]

    for k in range(4):
        @pl.when((step == 0) & (owner[me ^ k] == me))
        def _():
            for copy in copies(k):
                copy.start()

    out[...] = parent[...].astype(F32)

    for k in range(4):
        @pl.when((step == 0) & (owner[me ^ k] == me))
        def _():
            for copy in copies(k):
                copy.wait()

    for k in range(4):
        @pl.when(owner[me ^ k] == me)
        def _():
            for b in range(6):
                j = block_map[me ^ k, 8 * b + col] >> 3

                @pl.when(j >> 1 == step)
                def _():
                    for a in range(12):
                        i = block_map[me ^ k, 4 * a + here] >> 2
                        x = held[k, a * BLK : (a + 1) * BLK, b * BLK : (b + 1) * BLK]
                        out[block_at(i), block_at(j & 1)] += x.astype(F32)


def per_device(fronts, parents, parent_of, block_map):
    tile = lax.axis_index("tile")
    row, col = tile // 8, tile % 8
    a = fronts[0, 0]
    big = jax.ShapeDtypeStruct((1024, 1024), BF16)
    mid = jax.ShapeDtypeStruct((512, 512), F32)
    wide = jax.ShapeDtypeStruct((512, 1024), BF16)
    top_shape = jax.ShapeDtypeStruct((BLK, 256), BF16)
    piece = pltpu.VMEM((512, 512), BF16)
    quarter = pltpu.VMEM((512, 512), F32)
    strip = pltpu.VMEM((512, 1024), BF16)
    line = pltpu.VMEM((BLK, 1024), F32)
    block = pltpu.VMEM((BLK, BLK), F32)
    rows_t = pltpu.VMEM((160, BLK), F32)

    crossing = jnp.sum(jnp.where(parent_of // 2 != jnp.arange(4) // 2, 1 << jnp.arange(4), 0))
    def swap(x, k):
        return lax.ppermute(x, "tile", [(i, i ^ k) for i in range(32)])

    def call(kernel, name, flops, ins, outs, scratch):
        return pl.pallas_call(
            kernel,
            out_shape=outs,
            in_specs=[VMEM] * len(ins),
            out_specs=(VMEM,) * len(outs),
            scratch_shapes=scratch,
            compiler_params=PARAMS,
            cost_estimate=cost(flops, 8_000_000),
            name=name,
        )(*ins)

    def core_swap(x):
        return lax.ppermute(x, "front", [(i, i ^ 1) for i in range(4)])

    def cross(x):
        def branch(mask):
            pairs = [(i, i ^ 2) for i in range(4) if mask >> i & 1]
            return lambda v: lax.ppermute(v, "front", pairs) if pairs else jnp.zeros_like(v)

        return lax.switch(crossing, [branch(mask) for mask in range(16)], x)

    x_groups = [[4 * y + x for x in range(4)] for y in range(8)]
    row_groups = [[8 * r + c for c in range(8)] for r in range(4)]
    z_groups = [[i, i + 16] for i in range(16)]
    low_half = col < 4

    def column_swap(x):
        return jnp.concatenate([x] + [swap(x, 8 * k) for k in range(1, 4)], 0)

    def x_swap(x):
        return [x] + [swap(x, k) for k in range(1, 4)]

    q0 = a[:BLK, :BLK]
    other = swap(q0, 4)
    rest = a[BLK:512, :256]
    other, rest = lax.optimization_barrier((other, rest))
    q0 = column_swap(jnp.where(low_half, q0, other))
    far = swap(rest, 4)
    q0, far = lax.optimization_barrier((q0, far))
    q0 = x_swap(q0)
    lo = jnp.where(low_half, rest, far)
    hi = jnp.where(low_half, far, rest)
    q12 = jnp.concatenate(
        [lo[:BLK, :BLK], hi[:BLK, :BLK], lo[BLK : 2 * BLK, :BLK], hi[BLK : 2 * BLK, :BLK], lo[BLK : 2 * BLK, BLK:]], 1
    )
    q12 = column_swap(q12)
    trail = a[512:, :256].reshape(2, 2, 384, 256)
    half = col // 4
    near = lax.dynamic_index_in_dim(trail, half, 1, keepdims=False)
    away = lax.dynamic_index_in_dim(trail, 1 - half, 1, keepdims=False)
    side_top, side_low = a[:256, 256:], a[256:512, 256:]
    *q0, q12, lo, hi, away, side_low = lax.optimization_barrier((*q0, q12, lo, hi, away, side_low))
    q1, q2 = x_swap(q12[:, : 2 * BLK]), q12[:, 2 * BLK :]
    q3 = jnp.concatenate([lo[2 * BLK :, :BLK], hi[2 * BLK :, :BLK], lo[2 * BLK :, BLK:], hi[2 * BLK :, BLK:]], 1)
    q3 = lax.all_gather(q3, "tile", axis=0, axis_index_groups=x_groups)
    far = swap(away, 4)
    low_y = swap(side_low, 8)

    wa, top0 = call(kernel_a, "panel_a", 25_000_000_000, q0, (mid, top_shape), [quarter, block, rows_t])
    wa, q2, q3, far, low_y, *q1 = lax.optimization_barrier((wa, q2, q3, far, low_y, *q1))
    side_top = lax.all_gather(side_top, "tile", axis=0, axis_index_groups=z_groups)
    q2 = x_swap(q2)
    q3_y, q3_z = swap(q3, 8), swap(q3, 16)
    w0hi, w0lo, top1 = call(
        kernel_b,
        "panel_b",
        32_000_000_000,
        q1 + [wa],
        (big, big, top_shape),
        [quarter, quarter, quarter, piece, piece, line, block, rows_t],
    )
    w0hi, far, q3_y, side_top, *q2 = lax.optimization_barrier((w0hi, far, q3_y, side_top, *q2))
    q3 = [q3, q3_y, q3_z, swap(q3_y, 16)]
    both = jnp.concatenate([near, far], 2).reshape(2, 4, 96, 512)
    pieces = [
        lax.dynamic_index_in_dim(both, (col % 4) ^ k, 1, keepdims=False).reshape(192, 512) for k in range(4)
    ]
    pieces = pieces[:1] + [swap(pieces[k], k) for k in range(1, 4)]
    top_y = swap(side_top, 8)
    low_c, wc, top2 = call(
        kernel_c,
        "panel_c",
        35_000_000_000,
        q2 + [w0hi, w0lo],
        (wide, mid, top_shape),
        [quarter, strip, strip, pltpu.VMEM((BLK, 512), F32), block, rows_t],
    )
    wc, top_y, *rest = lax.optimization_barrier((wc, top_y, *pieces, *q3))
    pieces, q3 = rest[:4], rest[4:]
    low_z = [swap(x, 16) for x in (side_low, low_y)]
    sub = jax.ShapeDtypeStruct((2, 96, 1024), BF16)
    (first,) = call(
        functools.partial(rows_kernel, 0),
        "first_rows",
        1_200_000_000,
        pieces + [w0hi, w0lo],
        (sub,),
        [pltpu.VMEM((192, 1024), F32)],
    )
    l0 = lax.all_gather(first, "tile", axis=0, axis_index_groups=row_groups)
    low_d, w1hi, w1lo, top3 = call(
        kernel_d,
        "panel_d",
        38_000_000_000,
        q3 + [w0hi, w0lo, low_c, wc],
        (wide, big, big, top_shape),
        [quarter, quarter, quarter, piece, piece, strip, strip, line, block, rows_t],
    )
    w1hi, *low_z = lax.optimization_barrier((w1hi, *low_z))
    (second,) = call(
        functools.partial(rows_kernel, 1),
        "second_rows",
        1_700_000_000,
        pieces + [w1hi, w1lo, low_c, low_d, first],
        (sub,),
        [pltpu.VMEM((192, 1024), F32)],
    )
    pair = swap(second, 4)
    tall = jax.ShapeDtypeStruct((1024, 768), BF16)
    second, side_top = lax.optimization_barrier((second, side_top))
    t0, nhi, nlo = call(
        columns_first,
        "columns_first",
        9_000_000_000,
        [side_top, top_y, side_low, low_y, *low_z, w0hi, w0lo, low_c, low_d],
        (tall, tall, tall),
        [pltpu.VMEM((1024, 768), BF16)] * 2 + [pltpu.VMEM((1024, 768), F32)],
    )
    nhi, pair = lax.optimization_barrier((nhi, pair))
    later = jnp.stack([second[1], pair[1]])
    l1 = x_swap(jnp.stack([second[0], pair[0]]))
    (t1,) = call(
        columns_second, "columns_second", 9_000_000_000, [nhi, nlo, w1hi, w1lo], (tall,), []
    )
    t1, later = lax.optimization_barrier((t1, later))
    l1 = [l1, x_swap(later)]

    def update(h):
        def rows_of(k):
            return pl.BlockSpec((256, 256), lambda j: (2 + 3 * h + k, 1 + j))

        return pl.pallas_call(
            update_kernel,
            grid=(3,),
            out_shape=(
                jax.ShapeDtypeStruct((768, 768), BF16),
                jax.ShapeDtypeStruct((768, 256), BF16),
            ),
            in_specs=[
                pl.BlockSpec((8, 1, 96, 1024), lambda j: (0, h, 0, 0)),
                *[pl.BlockSpec((2, 96, 1024), lambda j: (0, 0, 0))] * 4,
                pl.BlockSpec((1024, 256), lambda j: (0, j)),
                pl.BlockSpec((1024, 256), lambda j: (0, j)),
                rows_of(0),
                rows_of(1),
                rows_of(2),
            ],
            out_specs=(
                pl.BlockSpec((768, 256), lambda j: (0, j)),
                pl.BlockSpec((768, 256), lambda j: (0, 0)),
            ),
            scratch_shapes=[pltpu.VMEM((768, 1024), BF16)],
            compiler_params=PARAMS,
            cost_estimate=cost(2_500_000_000, 9_000_000),
            name="update",
        )(l0, *l1[h], t0, t1, a, a, a)

    children, lower = [], []
    for h in range(2):
        if h:
            across, *l1[1] = lax.optimization_barrier((across, *l1[1]))
            children[0] = (*children[0][:2], across, core_swap(across))
        own, below = update(h)
        across = cross(own)
        children.append((own, core_swap(own), across, core_swap(across)))
        lower.append(below)
    factor = jnp.concatenate([top0, top1, top2, top3, *lower], 0)

    column = pl.BlockSpec((2048, 2 * BLK), lambda i, owner, block_map: (0, i))
    merged = pl.pallas_call(
        merge_kernel,
        grid_spec=pltpu.PrefetchScalarGridSpec(
            num_scalar_prefetch=2,
            grid=(4,),
            in_specs=[column] + [pl.BlockSpec(memory_space=pl.ANY)] * 8,
            out_specs=column,
            scratch_shapes=[pltpu.VMEM((4, 1536, 768), BF16), pltpu.SemaphoreType.DMA((4, 2))],
        ),
        out_shape=jax.ShapeDtypeStruct((2048, 1024), F32),
        compiler_params=PARAMS,
        cost_estimate=cost(10_000_000, 22_000_000),
        name="merge",
    )(parent_of, block_map, parents[0, 0], *[children[h][k] for k in range(4) for h in range(2)])
    return factor[None, None], merged[None, None]


def solution(mesh):
    return jax.shard_map(
        per_device,
        mesh=mesh,
        in_specs=(P("front", "tile", None, None), P("front", "tile", None, None), P(), P()),
        out_specs=(P("front", "tile", None, None), P("front", "tile", None, None)),
        check_vma=False,
    )
```

```python
import functools

import jax
import jax.numpy as jnp
from jax import lax
from jax.experimental import pallas as pl
from jax.experimental.pallas import tpu as pltpu
from jax.sharding import PartitionSpec as P

BLK = 128
F32 = jnp.float32
BF16 = jnp.bfloat16
NN = (((1,), (0,)), ((), ()))
NT = (((1,), (1,)), ((), ()))


def dot(a, b, dims):
    return lax.dot_general(a, b, dims, preferred_element_type=F32)


def split(x):
    hi = x.astype(BF16)
    return hi, (x - hi.astype(F32)).astype(BF16)


def dot3(a, b, dims):
    return dot(a[0], b[0], dims) + (dot(a[0], b[1], dims) + dot(a[1], b[0], dims))


def dotp(a, b, dims):
    return dot3(split(a), split(b), dims)


def lane_of(x, lane):
    return jnp.broadcast_to(x[:, lane : lane + 1], (8, BLK))


def factor_block(rows, out_ref, out_row, out_col, T):
    S = list(rows)
    lanes = lax.broadcasted_iota(jnp.int32, (8, BLK), 1)
    subs = lax.broadcasted_iota(jnp.int32, (8, BLK), 0)
    G = [(lanes == subs + 8 * v).astype(F32) for v in range(16)]
    for v0 in range(16):
        far = v0 + 3 + (v0 + 3) % 2
        far = far if far <= 12 else 16
        C = {v: [lane_of(S[v], 8 * v0 + j) for j in range(8)] for v in range(v0, far)}
        at = 80 * (v0 % 2)
        for n, x in enumerate([*C[v0], S[v0], G[v0]]):
            T[at + 8 * n : at + 8 * n + 8, :] = x

        def spread_row(n, i):
            return T[pl.ds(at + 8 * n + i, 8, stride=0), :]

        d = [[spread_row(j, i) if i >= j else None for j in range(8)] for i in range(8)]
        Rs = [spread_row(8, i) for i in range(8)]
        Rg = [spread_row(9, i) for i in range(8)]
        Cn = list(C[v0 + 1]) if v0 < 15 else None
        m = [[None] * 8 for _ in range(8)]
        Us, Ug = [None] * 8, [None] * 8
        wrows = None
        for j in range(8):
            rs = lax.rsqrt(d[j][j])
            p = rs * rs
            w = Rg[j] * rs
            wrows = w if j == 0 else jnp.where(subs == j, w, wrows)
            for i in range(j + 1, 8):
                m[i][j] = d[i][j] * p
            for i in range(j + 1, 8):
                for k in range(j + 1, i + 1):
                    d[i][k] = d[i][k] - m[i][j] * d[k][j]
            Us[j] = Rs[j] * p
            Ug[j] = Rg[j] * p
            if Cn is not None:
                S[v0 + 1] = S[v0 + 1] - Cn[j] * Us[j]
                G[v0 + 1] = G[v0 + 1] - Cn[j] * Ug[j]
            for i in range(j + 1, 8):
                Rs[i] = Rs[i] - m[i][j] * Rs[j]
                Rg[i] = Rg[i] - m[i][j] * Rg[j]
                if Cn is not None:
                    Cn[i] = Cn[i] - m[i][j] * Cn[j]
        out_ref[pl.ds(out_row + 8 * v0, 8), pl.ds(out_col, BLK)] = wrows
        if v0 < 14:
            for j in range(6, -1, -1):
                for i in range(j + 1, 8):
                    Us[j] = Us[j] - m[i][j] * Us[i]
                    Ug[j] = Ug[j] - m[i][j] * Ug[i]
            for v in range(v0 + 2, far):
                for j in range(8):
                    S[v] = S[v] - C[v][j] * Us[j]
                    G[v] = G[v] - C[v][j] * Ug[j]
            if far < 16:
                us, ug = Us[0], Ug[0]
                for j in range(1, 8):
                    us = jnp.where(subs == j, Us[j], us)
                    ug = jnp.where(subs == j, Ug[j], ug)
                parts = [jnp.concatenate([us, ug], 1)]
                if v0:
                    parts.insert(0, jnp.zeros((8 * v0, 2 * BLK), F32))
                parts.append(jnp.zeros((BLK - 8 * v0 - 8, 2 * BLK), F32))
                rank = split(jnp.concatenate(parts, 0))
                less = dot3(split(jnp.concatenate(S[far:], 0)), rank, NN)
                for v in range(far, 16):
                    at = slice(8 * (v - far), 8 * (v - far + 1))
                    S[v] = S[v] - less[at, :BLK]
                    G[v] = G[v] - less[at, BLK:]


def chol_inverse(A, W, Ls, T):
    pairs = A.shape[0] // 256
    W[...] = jnp.zeros(W.shape, F32)

    def step(kb, _):
        r0 = pl.multiple_of(kb * BLK, BLK)
        rows = [A[pl.ds(pl.multiple_of(r0 + 8 * v, 8), 8), pl.ds(r0, BLK)] for v in range(16)]
        factor_block(rows, W, r0, r0, T)

        @pl.when(kb % 2 == 0)
        def _():
            r1 = pl.multiple_of(r0 + BLK, BLK)
            low = dot3(split(A[pl.ds(r1, BLK), pl.ds(r0, BLK)]), split(W[pl.ds(r0, BLK), pl.ds(r0, BLK)]), NT)
            Ls[...] = low
            low = split(low)
            A[pl.ds(r1, BLK), pl.ds(r1, BLK)] -= dot3(low, low, NT)

        @pl.when(kb % 2 == 1)
        def _():
            q = pl.multiple_of(r0 - BLK, BLK)
            t = dot3(split(Ls[...]), split(W[pl.ds(q, BLK), pl.ds(q, BLK)]), NN)
            W[pl.ds(r0, BLK), pl.ds(q, BLK)] = -dot3(split(W[pl.ds(r0, BLK), pl.ds(r0, BLK)]), split(t), NN)

        for c in range(pairs):
            @pl.when(kb == 2 * c + 1)
            def _():
                lo, hi = 256 * c, 256 * (c + 1)
                wd = split(W[lo:hi, lo:hi])
                if c > 0:
                    W[lo:hi, :lo] = dot3(wd, split(W[lo:hi, :lo]), NN)
                if c < pairs - 1:
                    low = split(dot3(split(A[hi:, lo:hi]), wd, NT))
                    for n in range(c + 1, pairs):
                        a, b = 256 * n, 256 * (n + 1)
                        A[a:, a:b] -= dot3([x[a - hi :] for x in low], [x[a - hi : b - hi] for x in low], NT)
                    W[hi:, lo:hi] = -dot3(low, wd, NN)
                    if c > 0:
                        W[hi:, :lo] -= dot3(low, split(W[lo:hi, :lo]), NN)

        return 0

    lax.fori_loop(0, 2 * pairs, step, 0)


VMEM = pl.BlockSpec(memory_space=pltpu.VMEM)
PARAMS = pltpu.CompilerParams(vmem_limit_bytes=56 * 2**20)


def cost(flops, data):
    return pl.CostEstimate(flops=flops, bytes_accessed=data, transcendentals=0)


def position():
    tile = lax.axis_index("tile")
    return tile // 8, tile % 8


def times_inverse_t(x, w, put):
    for n in range(4):
        a, b = 256 * n, 256 * (n + 1)
        put(n, dot3((x[0][:, :b], x[1][:, :b]), (w[0][a:b, :b], w[1][a:b, :b]), NT))


def inverse_times(w, x, put):
    for n in range(4):
        a, b = 256 * n, 256 * (n + 1)
        put(n, dot3((w[0][a:b, :b], w[1][a:b, :b]), (x[0][:b], x[1][:b]), NN))


def store_split(hi, lo, index, x):
    h, l = split(x)
    hi[index] = h
    lo[index] = l


def block_at(index):
    return pl.ds(pl.multiple_of(index * BLK, BLK), BLK)


def finish_lower(whi, wlo, wa, low, wb):
    first, last = split(wa[...]), split(wb[...])
    below = split(-dot3(last, split(dot3(low, first, NN)), NN))
    for out, d0, d1, x in zip((whi, wlo), first, last, below):
        out[:512, :512] = d0
        out[:512, 512:] = jnp.zeros((512, 512), BF16)
        out[512:, :512] = x
        out[512:, 512:] = d1


def own_part(left, whi, wlo, index):
    return dot3(split(left), (whi[block_at(index), :], wlo[block_at(index), :]), NT)


def gather_first(pieces, row, col, A):
    for k in range(4):
        for n in range(4):
            A[block_at(((row ^ n) + 3) % 4), block_at((col % 4) ^ k)] = pieces[k][n * BLK : (n + 1) * BLK, :]


def kernel_a1(*refs):
    pieces = refs[:4]
    w, A, first, Ls, T = refs[4:]
    row, col = position()
    gather_first(pieces, row, col, A)
    first[...] = A[:256, :256]
    chol_inverse(first, w, Ls, T)


def kernel_a2(*refs):
    pieces = refs[:4]
    w, wa, top, A, last, wl, Ls, T = refs[4:]
    row, col = position()
    here = (row + 3) % 4
    gather_first(pieces, row, col, A)
    w11 = split(w[...])
    low = split(dot3(split(A[256:, :256]), w11, NT))
    last[...] = A[256:, 256:] - dot3(low, low, NT)
    chol_inverse(last, wl, Ls, T)
    wa[:256, :256] = w[...]
    wa[:256, 256:] = jnp.zeros((256, 256), F32)
    wa[256:, :256] = -dot3(split(wl[...]), split(dot3(low, w11, NN)), NN)
    wa[256:, 256:] = wl[...]
    own = dotp(A[block_at(here), :], wa[block_at(col % 4), :], NT)
    top[:, :BLK] = jnp.where((col < 4) & (here >= col), own, 0.0).astype(BF16)
    top[:, BLK:] = jnp.zeros((BLK, BLK), BF16)


def kernel_b(*refs):
    pieces = refs[:4]
    wa, whi, wlo, top, D, A, wb, lhi, llo, keep, Ls, T = refs[4:]
    row, col = position()
    here = (row + 3) % 4
    for k in range(4):
        for n in range(4):
            at = block_at(((row ^ n) + 3) % 4), block_at((col % 4) ^ k)
            D[at] = pieces[k][n * BLK : (n + 1) * BLK, :BLK]
            A[at] = pieces[k][n * BLK : (n + 1) * BLK, BLK:]
    keep[:, :512] = D[block_at(here), :]
    keep[:, 512:] = A[block_at(here), :]
    low = split(dot3(split(D[...]), split(wa[...]), NT))
    lhi[...], llo[...] = low
    A[...] -= dot3(low, low, NT)
    chol_inverse(A, wb, Ls, T)
    finish_lower(whi, wlo, wa, (lhi[...], llo[...]), wb)
    own = own_part(keep[...], whi, wlo, col)
    top[:, :BLK] = jnp.where(here + 4 >= col, own, 0.0).astype(BF16)
    top[:, BLK:] = jnp.zeros((BLK, BLK), BF16)


def place(src, i, x, xhi, xlo, blocks):
    rows = block_at(i)
    for half in range(2):
        store_split(xhi, xlo, (rows, block_at(4 * half + x)), src[:, half * BLK : (half + 1) * BLK])
    for n, ref in enumerate(blocks):
        ref[rows, block_at(x)] = src[:, (n + 2) * BLK : (n + 3) * BLK]


def spread(pieces, row, xhi, xlo, blocks):
    for k in range(4):
        for x in range(4):
            place(pieces[k][x], ((row ^ k) + 3) % 4, x, xhi, xlo, blocks)


def kernel_c(*refs):
    pieces = refs[:4]
    w0hi, w0lo, low, wc, top, A, xhi, xlo, keep, Ls, T = refs[4:]
    row, col = position()
    here = (row + 3) % 4
    for k in range(4):
        for n in range(4):
            place(pieces[k][n * BLK : (n + 1) * BLK, :], ((row ^ n) + 3) % 4, (col % 4) ^ k, xhi, xlo, [A])

    def put(n, x):
        low[:, 256 * n : 256 * (n + 1)] = x.astype(BF16)

    times_inverse_t((xhi, xlo), (w0hi, w0lo), put)
    A[...] -= dot(low[...], low[...], NT)
    keep[...] = A[block_at(here), :]
    chol_inverse(A, wc, Ls, T)
    own = dotp(keep[...], wc[block_at(col % 4), :], NT)
    top[:, :BLK] = low[block_at(here), block_at(col)]
    top[:, BLK:] = jnp.where((col < 4) & (here >= col), own, 0.0).astype(BF16)


def kernel_d(*refs):
    pieces = refs[:4]
    w0hi, w0lo, lowc, wc, low, whi, wlo, top, D, A, wd, lhi, llo, xhi, xlo, keep, Ls, T = refs[4:]
    row, col = position()
    here = (row + 3) % 4
    spread(pieces, row, xhi, xlo, [D, A])

    def put(n, x):
        low[:, 256 * n : 256 * (n + 1)] = x.astype(BF16)

    times_inverse_t((xhi, xlo), (w0hi, w0lo), put)
    D[...] -= dot(low[...], lowc[...], NT)
    A[...] -= dot(low[...], low[...], NT)
    keep[:, :512] = D[block_at(here), :]
    keep[:, 512:] = A[block_at(here), :]
    lower = split(dot3(split(D[...]), split(wc[...]), NT))
    lhi[...], llo[...] = lower
    A[...] -= dot3(lower, lower, NT)
    chol_inverse(A, wd, Ls, T)
    finish_lower(whi, wlo, wc, (lhi[...], llo[...]), wd)
    own = own_part(keep[...], whi, wlo, col)
    top[:, :BLK] = low[block_at(here), block_at(col)]
    top[:, BLK:] = jnp.where(here + 4 >= col, own, 0.0).astype(BF16)


def rows_kernel(panel, *refs):
    pieces, refs = refs[:4], refs[4:]
    row, col = position()
    if panel == 0:
        whi, wlo, out, x = refs
    else:
        whi, wlo, low_c, low_d, first, out, x = refs
    for k in range(4):
        for n in range(2):
            at = (2 * n + panel) * BLK
            x[:, block_at(col ^ k ^ (4 * n))] = pieces[k][:, at : at + BLK]
    v = x[...]
    if panel == 1:
        v = v - jnp.concatenate([dot(first[...].reshape(192, 1024), low[...], NT) for low in (low_c, low_d)], 1)

    def put(n, y):
        for h in range(2):
            out[h, :, 256 * n : 256 * (n + 1)] = y[96 * h : 96 * (h + 1)].astype(BF16)

    times_inverse_t(split(v), (whi, wlo), put)


def columns_first(*refs):
    top_z, top_y, low_y, low_z = refs[:4]
    w0hi, w0lo, low_c, low_d, t0, nhi, nlo, xhi, xlo, y = refs[4:]
    row, _ = position()
    for n in range(2):
        for top, side in ((top_z, row % 2), (top_y, 1 - row % 2)):
            at = (2 * n + side + 3) % 4
            for m in range(2):
                store_split(xhi, xlo, (block_at(4 * m + at), slice(None)), top[n, m * BLK : (m + 1) * BLK, :])
        for low, z in ((low_y, row // 2), (low_z, 1 - row // 2)):
            at = (2 * z + n + 3) % 4
            for m in range(2):
                y[block_at(4 * m + at), :] = low[n, m * BLK : (m + 1) * BLK, :]

    def put(n, v):
        t0[256 * n : 256 * (n + 1), :] = v.astype(BF16)

    inverse_times((w0hi, w0lo), (xhi, xlo), put)
    for n in range(2):
        at = slice(512 * n, 512 * (n + 1)), slice(None)
        store_split(nhi, nlo, at, y[at] - dot((low_c, low_d)[n][...], t0[...], NN))


def columns_second(nhi, nlo, whi, wlo, t1):
    def put(n, v):
        t1[256 * n : 256 * (n + 1), :] = v.astype(BF16)

    inverse_times((whi, wlo), (nhi, nlo), put)


def update_kernel(l0, *refs):
    pieces, (t0, t1, a0, a1, a2, out, factor, l1) = refs[:4], refs[4:]
    _, col = position()

    @pl.when(pl.program_id(0) == 0)
    def _():
        for k in range(4):
            for n in range(2):
                l1[pl.ds(pl.multiple_of((col ^ k ^ (4 * n)) * 96, 32), 96), :] = pieces[k][n]
        at = block_at(col)
        factor[:, :BLK] = l0[:, 0, :, at].reshape(768, BLK)
        factor[:, BLK:] = l1[:, at]

    total = dot(l0[:, 0].reshape(768, 1024), t0[...], NN) + dot(l1[...], t1[...], NN)
    for n, a in enumerate((a0, a1, a2)):
        at = slice(256 * n, 256 * (n + 1))
        out[at, :] = (a[...] - total[at]).astype(BF16)


def merge_kernel(owner, block_map, parent, *refs):
    children, (out, held, sem) = refs[:8], refs[8:]
    step = pl.program_id(0)
    me = lax.axis_index("front")
    row, col = position()
    here = (row + 3) % 4

    def copies(k):
        return [
            pltpu.make_async_copy(children[2 * k + h], held.at[k, pl.ds(768 * h, 768), :], sem.at[k, h])
            for h in range(2)
        ]

    for k in range(4):
        @pl.when((step == 0) & (owner[me ^ k] == me))
        def _():
            for copy in copies(k):
                copy.start()

    out[...] = parent[...].astype(F32)

    for k in range(4):
        @pl.when((step == 0) & (owner[me ^ k] == me))
        def _():
            for copy in copies(k):
                copy.wait()

    for k in range(4):
        @pl.when(owner[me ^ k] == me)
        def _():
            for b in range(6):
                j = block_map[me ^ k, 8 * b + col] >> 3

                @pl.when(j >> 1 == step)
                def _():
                    for a in range(12):
                        i = block_map[me ^ k, 4 * a + here] >> 2
                        x = held[k, a * BLK : (a + 1) * BLK, b * BLK : (b + 1) * BLK]
                        out[block_at(i), block_at(j & 1)] += x.astype(F32)


def per_device(fronts, parents, parent_of, block_map):
    tile = lax.axis_index("tile")
    row, col = tile // 8, tile % 8
    a = fronts[0, 0]
    big = jax.ShapeDtypeStruct((1024, 1024), BF16)
    mid = jax.ShapeDtypeStruct((512, 512), F32)
    wide = jax.ShapeDtypeStruct((512, 1024), BF16)
    top_shape = jax.ShapeDtypeStruct((BLK, 256), BF16)
    piece = pltpu.VMEM((512, 512), BF16)
    quarter = pltpu.VMEM((512, 512), F32)
    strip = pltpu.VMEM((512, 1024), BF16)
    line = pltpu.VMEM((BLK, 1024), F32)
    block = pltpu.VMEM((BLK, BLK), F32)
    rows_t = pltpu.VMEM((160, BLK), F32)

    crossing = jnp.sum(jnp.where(parent_of // 2 != jnp.arange(4) // 2, 1 << jnp.arange(4), 0))
    def swap(x, k):
        return lax.ppermute(x, "tile", [(i, i ^ k) for i in range(32)])

    def call(kernel, name, flops, ins, outs, scratch):
        return pl.pallas_call(
            kernel,
            out_shape=outs,
            in_specs=[VMEM] * len(ins),
            out_specs=(VMEM,) * len(outs),
            scratch_shapes=scratch,
            compiler_params=PARAMS,
            cost_estimate=cost(flops, 8_000_000),
            name=name,
        )(*ins)

    def core_swap(x):
        return lax.ppermute(x, "front", [(i, i ^ 1) for i in range(4)])

    def cross(x):
        def branch(mask):
            pairs = [(i, i ^ 2) for i in range(4) if mask >> i & 1]
            return lambda v: lax.ppermute(v, "front", pairs) if pairs else jnp.zeros_like(v)

        return lax.switch(crossing, [branch(mask) for mask in range(16)], x)

    x_groups = [[4 * y + x for x in range(4)] for y in range(8)]
    row_groups = [[8 * r + c for c in range(8)] for r in range(4)]
    y_groups = [[i, i + 8] for i in range(32) if not i & 8]
    z_groups = [[i, i + 16] for i in range(16)]
    low_half = col < 4

    def column_swap(x):
        return jnp.concatenate([x] + [swap(x, 8 * k) for k in range(1, 4)], 0)

    def x_swap(x):
        return [x] + [swap(x, k) for k in range(1, 4)]

    q0 = a[:BLK, :BLK]
    q0 = column_swap(jnp.where(low_half, q0, swap(q0, 4)))
    q0, rest = lax.optimization_barrier((q0, a[BLK:512, :256]))
    q0 = x_swap(q0)
    far = swap(rest, 4)
    lo = jnp.where(low_half, rest, far)
    hi = jnp.where(low_half, far, rest)
    q12 = jnp.concatenate(
        [lo[:BLK, :BLK], hi[:BLK, :BLK], lo[BLK : 2 * BLK, :BLK], hi[BLK : 2 * BLK, :BLK], lo[BLK : 2 * BLK, BLK:]], 1
    )
    q12 = column_swap(q12)
    q3 = jnp.concatenate([lo[2 * BLK :, :BLK], hi[2 * BLK :, :BLK], lo[2 * BLK :, BLK:], hi[2 * BLK :, BLK:]], 1)
    q3 = lax.all_gather(q3, "tile", axis=0, axis_index_groups=x_groups)
    trail = a[512:, :256].reshape(2, 2, 384, 256)
    half = col // 4
    near = lax.dynamic_index_in_dim(trail, half, 1, keepdims=False)
    away = lax.dynamic_index_in_dim(trail, 1 - half, 1, keepdims=False)
    side_top, side_low = a[:256, 256:], a[256:512, 256:]
    small = pltpu.VMEM((256, 256), F32)

    (w11,) = call(
        kernel_a1,
        "panel_a1",
        20_000_000_000,
        q0,
        (jax.ShapeDtypeStruct((256, 256), F32),),
        [quarter, small, block, rows_t],
    )
    w11, q12, away, side_top = lax.optimization_barrier((w11, q12, away, side_top))
    q1, q2 = x_swap(q12[:, : 2 * BLK]), q12[:, 2 * BLK :]
    far = swap(away, 4)
    side_top = lax.all_gather(side_top, "tile", axis=0, axis_index_groups=z_groups)
    wa, top0 = call(
        kernel_a2, "panel_a2", 20_000_000_000, q0 + [w11], (mid, top_shape), [quarter, small, small, block, rows_t]
    )
    wa, q2, q3, far, side_low, *q1 = lax.optimization_barrier((wa, q2, q3, far, side_low, *q1))
    low_y = lax.all_gather(side_low, "tile", axis=0, axis_index_groups=y_groups)
    q2 = x_swap(q2)
    q3_y, q3_z = swap(q3, 8), swap(q3, 16)
    w0hi, w0lo, top1 = call(
        kernel_b,
        "panel_b",
        32_000_000_000,
        q1 + [wa],
        (big, big, top_shape),
        [quarter, quarter, quarter, piece, piece, line, block, rows_t],
    )
    w0hi, far, q3_y, side_top, *q2 = lax.optimization_barrier((w0hi, far, q3_y, side_top, *q2))
    q3 = [q3, q3_y, q3_z, swap(q3_y, 16)]
    both = jnp.concatenate([near, far], 2).reshape(2, 4, 96, 512)
    pieces = [
        lax.dynamic_index_in_dim(both, (col % 4) ^ k, 1, keepdims=False).reshape(192, 512) for k in range(4)
    ]
    pieces = pieces[:1] + [swap(pieces[k], k) for k in range(1, 4)]
    top_y = swap(side_top, 8)
    low_c, wc, top2 = call(
        kernel_c,
        "panel_c",
        35_000_000_000,
        q2 + [w0hi, w0lo],
        (wide, mid, top_shape),
        [quarter, strip, strip, pltpu.VMEM((BLK, 512), F32), block, rows_t],
    )
    wc, top_y, low_y, *rest = lax.optimization_barrier((wc, top_y, low_y, *pieces, *q3))
    pieces, q3 = rest[:4], rest[4:]
    low_z = swap(low_y, 16)
    sub = jax.ShapeDtypeStruct((2, 96, 1024), BF16)
    (first,) = call(
        functools.partial(rows_kernel, 0),
        "first_rows",
        1_200_000_000,
        pieces + [w0hi, w0lo],
        (sub,),
        [pltpu.VMEM((192, 1024), F32)],
    )
    l0 = lax.all_gather(first, "tile", axis=0, axis_index_groups=row_groups)
    low_d, w1hi, w1lo, top3 = call(
        kernel_d,
        "panel_d",
        38_000_000_000,
        q3 + [w0hi, w0lo, low_c, wc],
        (wide, big, big, top_shape),
        [quarter, quarter, quarter, piece, piece, strip, strip, line, block, rows_t],
    )
    w1hi, low_z = lax.optimization_barrier((w1hi, low_z))
    (second,) = call(
        functools.partial(rows_kernel, 1),
        "second_rows",
        1_700_000_000,
        pieces + [w1hi, w1lo, low_c, low_d, first],
        (sub,),
        [pltpu.VMEM((192, 1024), F32)],
    )
    pair = swap(second, 4)
    tall = jax.ShapeDtypeStruct((1024, 768), BF16)
    second, side_top = lax.optimization_barrier((second, side_top))
    t0, nhi, nlo = call(
        columns_first,
        "columns_first",
        9_000_000_000,
        [side_top, top_y, low_y, low_z, w0hi, w0lo, low_c, low_d],
        (tall, tall, tall),
        [pltpu.VMEM((1024, 768), BF16)] * 2 + [pltpu.VMEM((1024, 768), F32)],
    )
    nhi, pair = lax.optimization_barrier((nhi, pair))
    later = jnp.stack([second[1], pair[1]])
    l1 = x_swap(jnp.stack([second[0], pair[0]]))
    (t1,) = call(
        columns_second, "columns_second", 9_000_000_000, [nhi, nlo, w1hi, w1lo], (tall,), []
    )
    l1 = [l1]

    def update(h):
        def rows_of(k):
            return pl.BlockSpec((256, 256), lambda j: (2 + 3 * h + k, 1 + j))

        return pl.pallas_call(
            update_kernel,
            grid=(3,),
            out_shape=(
                jax.ShapeDtypeStruct((768, 768), BF16),
                jax.ShapeDtypeStruct((768, 256), BF16),
            ),
            in_specs=[
                pl.BlockSpec((8, 1, 96, 1024), lambda j: (0, h, 0, 0)),
                *[pl.BlockSpec((2, 96, 1024), lambda j: (0, 0, 0))] * 4,
                pl.BlockSpec((1024, 256), lambda j: (0, j)),
                pl.BlockSpec((1024, 256), lambda j: (0, j)),
                rows_of(0),
                rows_of(1),
                rows_of(2),
            ],
            out_specs=(
                pl.BlockSpec((768, 256), lambda j: (0, j)),
                pl.BlockSpec((768, 256), lambda j: (0, 0)),
            ),
            scratch_shapes=[pltpu.VMEM((768, 1024), BF16)],
            compiler_params=PARAMS,
            cost_estimate=cost(2_500_000_000, 9_000_000),
            name="update",
        )(l0, *l1[h], t0, t1, a, a, a)

    children, lower = [], []
    for h in range(2):
        if h:
            across, *l1[1] = lax.optimization_barrier((across, *l1[1]))
            children[0] = (*children[0][:2], across, core_swap(across))
        own, below = update(h)
        if not h:
            own, later = lax.optimization_barrier((own, later))
            l1.append(x_swap(later))
        across = cross(own)
        children.append((own, core_swap(own), across, core_swap(across)))
        lower.append(below)
    factor = jnp.concatenate([top0, top1, top2, top3, *lower], 0)

    column = pl.BlockSpec((2048, 2 * BLK), lambda i, owner, block_map: (0, i))
    merged = pl.pallas_call(
        merge_kernel,
        grid_spec=pltpu.PrefetchScalarGridSpec(
            num_scalar_prefetch=2,
            grid=(4,),
            in_specs=[column] + [pl.BlockSpec(memory_space=pl.ANY)] * 8,
            out_specs=column,
            scratch_shapes=[pltpu.VMEM((4, 1536, 768), BF16), pltpu.SemaphoreType.DMA((4, 2))],
        ),
        out_shape=jax.ShapeDtypeStruct((2048, 1024), F32),
        compiler_params=PARAMS,
        cost_estimate=cost(10_000_000, 22_000_000),
        name="merge",
    )(parent_of, block_map, parents[0, 0], *[children[h][k] for k in range(4) for h in range(2)])
    return factor[None, None], merged[None, None]


def solution(mesh):
    return jax.shard_map(
        per_device,
        mesh=mesh,
        in_specs=(P("front", "tile", None, None), P("front", "tile", None, None), P(), P()),
        out_specs=(P("front", "tile", None, None), P("front", "tile", None, None)),
        check_vma=False,
    )
```

```python
import functools

import jax
import jax.numpy as jnp
from jax import lax
from jax.experimental import pallas as pl
from jax.experimental.pallas import tpu as pltpu
from jax.sharding import PartitionSpec as P

BLK = 128
F32 = jnp.float32
BF16 = jnp.bfloat16
NN = (((1,), (0,)), ((), ()))
NT = (((1,), (1,)), ((), ()))


def dot(a, b, dims):
    return lax.dot_general(a, b, dims, preferred_element_type=F32)


def split(x):
    hi = x.astype(BF16)
    return hi, (x - hi.astype(F32)).astype(BF16)


def dot3(a, b, dims):
    return dot(a[0], b[0], dims) + (dot(a[0], b[1], dims) + dot(a[1], b[0], dims))


def dotp(a, b, dims):
    return dot3(split(a), split(b), dims)


def lane_of(x, lane):
    return jnp.broadcast_to(x[:, lane : lane + 1], (8, BLK))


def factor_block(rows, out_ref, out_row, out_col, T):
    S = list(rows)
    lanes = lax.broadcasted_iota(jnp.int32, (8, BLK), 1)
    subs = lax.broadcasted_iota(jnp.int32, (8, BLK), 0)
    G = [(lanes == subs + 8 * v).astype(F32) for v in range(16)]
    for v0 in range(16):
        far = v0 + 3 + (v0 + 3) % 2
        far = far if far <= 12 else 16
        C = {v: [lane_of(S[v], 8 * v0 + j) for j in range(8)] for v in range(v0, far)}
        at = 80 * (v0 % 2)
        for n, x in enumerate([*C[v0], S[v0], G[v0]]):
            T[at + 8 * n : at + 8 * n + 8, :] = x

        def spread_row(n, i):
            return T[pl.ds(at + 8 * n + i, 8, stride=0), :]

        d = [[spread_row(j, i) if i >= j else None for j in range(8)] for i in range(8)]
        Rs = [spread_row(8, i) for i in range(8)]
        Rg = [spread_row(9, i) for i in range(8)]
        Cn = list(C[v0 + 1]) if v0 < 15 else None
        m = [[None] * 8 for _ in range(8)]
        Us, Ug = [None] * 8, [None] * 8
        wrows = None
        for j in range(8):
            rs = lax.rsqrt(d[j][j])
            p = rs * rs
            w = Rg[j] * rs
            wrows = w if j == 0 else jnp.where(subs == j, w, wrows)
            for i in range(j + 1, 8):
                m[i][j] = d[i][j] * p
            for i in range(j + 1, 8):
                for k in range(j + 1, i + 1):
                    d[i][k] = d[i][k] - m[i][j] * d[k][j]
            Us[j] = Rs[j] * p
            Ug[j] = Rg[j] * p
            if Cn is not None:
                S[v0 + 1] = S[v0 + 1] - Cn[j] * Us[j]
                G[v0 + 1] = G[v0 + 1] - Cn[j] * Ug[j]
            for i in range(j + 1, 8):
                Rs[i] = Rs[i] - m[i][j] * Rs[j]
                Rg[i] = Rg[i] - m[i][j] * Rg[j]
                if Cn is not None:
                    Cn[i] = Cn[i] - m[i][j] * Cn[j]
        out_ref[pl.ds(out_row + 8 * v0, 8), pl.ds(out_col, BLK)] = wrows
        if v0 < 14:
            for j in range(6, -1, -1):
                for i in range(j + 1, 8):
                    Us[j] = Us[j] - m[i][j] * Us[i]
                    Ug[j] = Ug[j] - m[i][j] * Ug[i]
            for v in range(v0 + 2, far):
                for j in range(8):
                    S[v] = S[v] - C[v][j] * Us[j]
                    G[v] = G[v] - C[v][j] * Ug[j]
            if far < 16:
                us, ug = Us[0], Ug[0]
                for j in range(1, 8):
                    us = jnp.where(subs == j, Us[j], us)
                    ug = jnp.where(subs == j, Ug[j], ug)
                parts = [jnp.concatenate([us, ug], 1)]
                if v0:
                    parts.insert(0, jnp.zeros((8 * v0, 2 * BLK), F32))
                parts.append(jnp.zeros((BLK - 8 * v0 - 8, 2 * BLK), F32))
                rank = split(jnp.concatenate(parts, 0))
                less = dot3(split(jnp.concatenate(S[far:], 0)), rank, NN)
                for v in range(far, 16):
                    at = slice(8 * (v - far), 8 * (v - far + 1))
                    S[v] = S[v] - less[at, :BLK]
                    G[v] = G[v] - less[at, BLK:]


def chol_inverse(A, W, Ls, T):
    pairs = A.shape[0] // 256
    W[...] = jnp.zeros(W.shape, F32)

    def step(kb, _):
        r0 = pl.multiple_of(kb * BLK, BLK)
        rows = [A[pl.ds(pl.multiple_of(r0 + 8 * v, 8), 8), pl.ds(r0, BLK)] for v in range(16)]
        factor_block(rows, W, r0, r0, T)

        @pl.when(kb % 2 == 0)
        def _():
            r1 = pl.multiple_of(r0 + BLK, BLK)
            low = dot3(split(A[pl.ds(r1, BLK), pl.ds(r0, BLK)]), split(W[pl.ds(r0, BLK), pl.ds(r0, BLK)]), NT)
            Ls[...] = low
            low = split(low)
            A[pl.ds(r1, BLK), pl.ds(r1, BLK)] -= dot3(low, low, NT)

        @pl.when(kb % 2 == 1)
        def _():
            q = pl.multiple_of(r0 - BLK, BLK)
            t = dot3(split(Ls[...]), split(W[pl.ds(q, BLK), pl.ds(q, BLK)]), NN)
            W[pl.ds(r0, BLK), pl.ds(q, BLK)] = -dot3(split(W[pl.ds(r0, BLK), pl.ds(r0, BLK)]), split(t), NN)

        for c in range(pairs):
            @pl.when(kb == 2 * c + 1)
            def _():
                lo, hi = 256 * c, 256 * (c + 1)
                wd = split(W[lo:hi, lo:hi])
                if c > 0:
                    W[lo:hi, :lo] = dot3(wd, split(W[lo:hi, :lo]), NN)
                if c < pairs - 1:
                    low = split(dot3(split(A[hi:, lo:hi]), wd, NT))
                    for n in range(c + 1, pairs):
                        a, b = 256 * n, 256 * (n + 1)
                        A[a:, a:b] -= dot3([x[a - hi :] for x in low], [x[a - hi : b - hi] for x in low], NT)
                    W[hi:, lo:hi] = -dot3(low, wd, NN)
                    if c > 0:
                        W[hi:, :lo] -= dot3(low, split(W[lo:hi, :lo]), NN)

        return 0

    lax.fori_loop(0, 2 * pairs, step, 0)


VMEM = pl.BlockSpec(memory_space=pltpu.VMEM)
PARAMS = pltpu.CompilerParams(vmem_limit_bytes=56 * 2**20)


def cost(flops, data):
    return pl.CostEstimate(flops=flops, bytes_accessed=data, transcendentals=0)


def position():
    tile = lax.axis_index("tile")
    return tile // 8, tile % 8


def times_inverse_t(x, w, put):
    for n in range(4):
        a, b = 256 * n, 256 * (n + 1)
        put(n, dot3((x[0][:, :b], x[1][:, :b]), (w[0][a:b, :b], w[1][a:b, :b]), NT))


def inverse_times(w, x, put):
    for n in range(4):
        a, b = 256 * n, 256 * (n + 1)
        put(n, dot3((w[0][a:b, :b], w[1][a:b, :b]), (x[0][:b], x[1][:b]), NN))


def store_split(hi, lo, index, x):
    h, l = split(x)
    hi[index] = h
    lo[index] = l


def block_at(index):
    return pl.ds(pl.multiple_of(index * BLK, BLK), BLK)


def finish_lower(whi, wlo, wa, low, wb):
    first, last = split(wa[...]), split(wb[...])
    below = split(-dot3(last, split(dot3(low, first, NN)), NN))
    for out, d0, d1, x in zip((whi, wlo), first, last, below):
        out[:512, :512] = d0
        out[:512, 512:] = jnp.zeros((512, 512), BF16)
        out[512:, :512] = x
        out[512:, 512:] = d1


def own_part(left, whi, wlo, index):
    return dot3(split(left), (whi[block_at(index), :], wlo[block_at(index), :]), NT)


def gather_first(pieces, row, col, A):
    for k in range(4):
        for n in range(4):
            A[block_at(((row ^ n) + 3) % 4), block_at((col % 4) ^ k)] = pieces[k][n * BLK : (n + 1) * BLK, :]


def kernel_a1(*refs):
    pieces = refs[:4]
    w, A, first, Ls, T = refs[4:]
    row, col = position()
    gather_first(pieces, row, col, A)
    first[...] = A[:256, :256]
    chol_inverse(first, w, Ls, T)


def kernel_a2(*refs):
    pieces = refs[:4]
    w, wa, top, A, last, wl, Ls, T = refs[4:]
    row, col = position()
    here = (row + 3) % 4
    gather_first(pieces, row, col, A)
    w11 = split(w[...])
    low = split(dot3(split(A[256:, :256]), w11, NT))
    last[...] = A[256:, 256:] - dot3(low, low, NT)
    chol_inverse(last, wl, Ls, T)
    wa[:256, :256] = w[...]
    wa[:256, 256:] = jnp.zeros((256, 256), F32)
    wa[256:, :256] = -dot3(split(wl[...]), split(dot3(low, w11, NN)), NN)
    wa[256:, 256:] = wl[...]
    own = dotp(A[block_at(here), :], wa[block_at(col % 4), :], NT)
    top[:, :BLK] = jnp.where((col < 4) & (here >= col), own, 0.0).astype(BF16)
    top[:, BLK:] = jnp.zeros((BLK, BLK), BF16)


def kernel_b(*refs):
    pieces = refs[:4]
    wa, whi, wlo, top, D, A, wb, lhi, llo, keep, Ls, T = refs[4:]
    row, col = position()
    here = (row + 3) % 4
    for k in range(4):
        for n in range(4):
            at = block_at(((row ^ n) + 3) % 4), block_at((col % 4) ^ k)
            D[at] = pieces[k][n * BLK : (n + 1) * BLK, :BLK]
            A[at] = pieces[k][n * BLK : (n + 1) * BLK, BLK:]
    keep[:, :512] = D[block_at(here), :]
    keep[:, 512:] = A[block_at(here), :]
    low = split(dot3(split(D[...]), split(wa[...]), NT))
    lhi[...], llo[...] = low
    A[...] -= dot3(low, low, NT)
    chol_inverse(A, wb, Ls, T)
    finish_lower(whi, wlo, wa, (lhi[...], llo[...]), wb)
    own = own_part(keep[...], whi, wlo, col)
    top[:, :BLK] = jnp.where(here + 4 >= col, own, 0.0).astype(BF16)
    top[:, BLK:] = jnp.zeros((BLK, BLK), BF16)


def place(src, i, x, xhi, xlo, blocks):
    rows = block_at(i)
    for half in range(2):
        store_split(xhi, xlo, (rows, block_at(4 * half + x)), src[:, half * BLK : (half + 1) * BLK])
    for n, ref in enumerate(blocks):
        ref[rows, block_at(x)] = src[:, (n + 2) * BLK : (n + 3) * BLK]


def spread(pieces, row, xhi, xlo, blocks):
    for k in range(4):
        for x in range(4):
            place(pieces[k][x], ((row ^ k) + 3) % 4, x, xhi, xlo, blocks)


def kernel_c(*refs):
    pieces = refs[:4]
    w0hi, w0lo, low, wc, top, A, xhi, xlo, keep, Ls, T = refs[4:]
    row, col = position()
    here = (row + 3) % 4
    for k in range(4):
        for n in range(4):
            place(pieces[k][n * BLK : (n + 1) * BLK, :], ((row ^ n) + 3) % 4, (col % 4) ^ k, xhi, xlo, [A])

    def put(n, x):
        low[:, 256 * n : 256 * (n + 1)] = x.astype(BF16)

    times_inverse_t((xhi, xlo), (w0hi, w0lo), put)
    A[...] -= dot(low[...], low[...], NT)
    keep[...] = A[block_at(here), :]
    chol_inverse(A, wc, Ls, T)
    own = dotp(keep[...], wc[block_at(col % 4), :], NT)
    top[:, :BLK] = low[block_at(here), block_at(col)]
    top[:, BLK:] = jnp.where((col < 4) & (here >= col), own, 0.0).astype(BF16)


def kernel_d(*refs):
    pieces = refs[:4]
    w0hi, w0lo, lowc, wc, low, whi, wlo, top, D, A, wd, lhi, llo, xhi, xlo, keep, Ls, T = refs[4:]
    row, col = position()
    here = (row + 3) % 4
    spread(pieces, row, xhi, xlo, [D, A])

    def put(n, x):
        low[:, 256 * n : 256 * (n + 1)] = x.astype(BF16)

    times_inverse_t((xhi, xlo), (w0hi, w0lo), put)
    D[...] -= dot(low[...], lowc[...], NT)
    A[...] -= dot(low[...], low[...], NT)
    keep[:, :512] = D[block_at(here), :]
    keep[:, 512:] = A[block_at(here), :]
    lower = split(dot3(split(D[...]), split(wc[...]), NT))
    lhi[...], llo[...] = lower
    A[...] -= dot3(lower, lower, NT)
    chol_inverse(A, wd, Ls, T)
    finish_lower(whi, wlo, wc, (lhi[...], llo[...]), wd)
    own = own_part(keep[...], whi, wlo, col)
    top[:, :BLK] = low[block_at(here), block_at(col)]
    top[:, BLK:] = jnp.where(here + 4 >= col, own, 0.0).astype(BF16)


def rows_kernel(panel, *refs):
    pieces, refs = refs[:4], refs[4:]
    row, col = position()
    if panel == 0:
        whi, wlo, out, x = refs
    else:
        whi, wlo, low_c, low_d, first, out, x = refs
    for k in range(4):
        for n in range(2):
            at = (2 * n + panel) * BLK
            x[:, block_at(col ^ k ^ (4 * n))] = pieces[k][:, at : at + BLK]
    v = x[...]
    if panel == 1:
        v = v - jnp.concatenate([dot(first[...].reshape(192, 1024), low[...], NT) for low in (low_c, low_d)], 1)

    def put(n, y):
        for h in range(2):
            out[h, :, 256 * n : 256 * (n + 1)] = y[96 * h : 96 * (h + 1)].astype(BF16)

    times_inverse_t(split(v), (whi, wlo), put)


def columns_first(*refs):
    top_z, top_y = refs[:2]
    lows = refs[2:6]
    w0hi, w0lo, low_c, low_d, t0, nhi, nlo, xhi, xlo, y = refs[6:]
    row, _ = position()
    for n in range(2):
        for top, side in ((top_z, row % 2), (top_y, 1 - row % 2)):
            at = (2 * n + side + 3) % 4
            for m in range(2):
                store_split(xhi, xlo, (block_at(4 * m + at), slice(None)), top[n, m * BLK : (m + 1) * BLK, :])
    for k in range(4):
        at = ((row ^ k) + 3) % 4
        for m in range(2):
            y[block_at(4 * m + at), :] = lows[k][m * BLK : (m + 1) * BLK, :]

    def put(n, v):
        t0[256 * n : 256 * (n + 1), :] = v.astype(BF16)

    inverse_times((w0hi, w0lo), (xhi, xlo), put)
    for n in range(2):
        at = slice(512 * n, 512 * (n + 1)), slice(None)
        store_split(nhi, nlo, at, y[at] - dot((low_c, low_d)[n][...], t0[...], NN))


def columns_second(nhi, nlo, whi, wlo, t1):
    def put(n, v):
        t1[256 * n : 256 * (n + 1), :] = v.astype(BF16)

    inverse_times((whi, wlo), (nhi, nlo), put)


def update_kernel(l0, *refs):
    pieces, (t0, t1, a0, a1, a2, out, factor, l1) = refs[:4], refs[4:]
    _, col = position()

    @pl.when(pl.program_id(0) == 0)
    def _():
        for k in range(4):
            for n in range(2):
                l1[pl.ds(pl.multiple_of((col ^ k ^ (4 * n)) * 96, 32), 96), :] = pieces[k][n]
        at = block_at(col)
        factor[:, :BLK] = l0[:, 0, :, at].reshape(768, BLK)
        factor[:, BLK:] = l1[:, at]

    total = dot(l0[:, 0].reshape(768, 1024), t0[...], NN) + dot(l1[...], t1[...], NN)
    for n, a in enumerate((a0, a1, a2)):
        at = slice(256 * n, 256 * (n + 1))
        out[at, :] = (a[...] - total[at]).astype(BF16)


def merge_kernel(owner, block_map, parent, *refs):
    children, (out, held, sem) = refs[:8], refs[8:]
    step = pl.program_id(0)
    me = lax.axis_index("front")
    row, col = position()
    here = (row + 3) % 4

    def copies(k):
        return [
            pltpu.make_async_copy(children[2 * k + h], held.at[k, pl.ds(768 * h, 768), :], sem.at[k, h])
            for h in range(2)
        ]

    for k in range(4):
        @pl.when((step == 0) & (owner[me ^ k] == me))
        def _():
            for copy in copies(k):
                copy.start()

    out[...] = parent[...].astype(F32)

    for k in range(4):
        @pl.when((step == 0) & (owner[me ^ k] == me))
        def _():
            for copy in copies(k):
                copy.wait()

    for k in range(4):
        @pl.when(owner[me ^ k] == me)
        def _():
            for b in range(6):
                j = block_map[me ^ k, 8 * b + col] >> 3

                @pl.when(j >> 1 == step)
                def _():
                    for a in range(12):
                        i = block_map[me ^ k, 4 * a + here] >> 2
                        x = held[k, a * BLK : (a + 1) * BLK, b * BLK : (b + 1) * BLK]
                        out[block_at(i), block_at(j & 1)] += x.astype(F32)


def per_device(fronts, parents, parent_of, block_map):
    tile = lax.axis_index("tile")
    row, col = tile // 8, tile % 8
    a = fronts[0, 0]
    big = jax.ShapeDtypeStruct((1024, 1024), BF16)
    mid = jax.ShapeDtypeStruct((512, 512), F32)
    wide = jax.ShapeDtypeStruct((512, 1024), BF16)
    top_shape = jax.ShapeDtypeStruct((BLK, 256), BF16)
    piece = pltpu.VMEM((512, 512), BF16)
    quarter = pltpu.VMEM((512, 512), F32)
    strip = pltpu.VMEM((512, 1024), BF16)
    line = pltpu.VMEM((BLK, 1024), F32)
    block = pltpu.VMEM((BLK, BLK), F32)
    rows_t = pltpu.VMEM((160, BLK), F32)

    crossing = jnp.sum(jnp.where(parent_of // 2 != jnp.arange(4) // 2, 1 << jnp.arange(4), 0))
    def swap(x, k):
        return lax.ppermute(x, "tile", [(i, i ^ k) for i in range(32)])

    def call(kernel, name, flops, ins, outs, scratch):
        return pl.pallas_call(
            kernel,
            out_shape=outs,
            in_specs=[VMEM] * len(ins),
            out_specs=(VMEM,) * len(outs),
            scratch_shapes=scratch,
            compiler_params=PARAMS,
            cost_estimate=cost(flops, 8_000_000),
            name=name,
        )(*ins)

    def core_swap(x):
        return lax.ppermute(x, "front", [(i, i ^ 1) for i in range(4)])

    def cross(x):
        def branch(mask):
            pairs = [(i, i ^ 2) for i in range(4) if mask >> i & 1]
            return lambda v: lax.ppermute(v, "front", pairs) if pairs else jnp.zeros_like(v)

        return lax.switch(crossing, [branch(mask) for mask in range(16)], x)

    x_groups = [[4 * y + x for x in range(4)] for y in range(8)]
    row_groups = [[8 * r + c for c in range(8)] for r in range(4)]
    z_groups = [[i, i + 16] for i in range(16)]
    low_half = col < 4

    def column_swap(x):
        return jnp.concatenate([x] + [swap(x, 8 * k) for k in range(1, 4)], 0)

    def x_swap(x):
        return [x] + [swap(x, k) for k in range(1, 4)]

    q0 = a[:BLK, :BLK]
    q0 = column_swap(jnp.where(low_half, q0, swap(q0, 4)))
    q0, rest = lax.optimization_barrier((q0, a[BLK:512, :256]))
    q0 = x_swap(q0)
    far = swap(rest, 4)
    lo = jnp.where(low_half, rest, far)
    hi = jnp.where(low_half, far, rest)
    q12 = jnp.concatenate(
        [lo[:BLK, :BLK], hi[:BLK, :BLK], lo[BLK : 2 * BLK, :BLK], hi[BLK : 2 * BLK, :BLK], lo[BLK : 2 * BLK, BLK:]], 1
    )
    q12 = column_swap(q12)
    q3 = jnp.concatenate([lo[2 * BLK :, :BLK], hi[2 * BLK :, :BLK], lo[2 * BLK :, BLK:], hi[2 * BLK :, BLK:]], 1)
    q3 = lax.all_gather(q3, "tile", axis=0, axis_index_groups=x_groups)
    trail = a[512:, :256].reshape(2, 2, 384, 256)
    half = col // 4
    near = lax.dynamic_index_in_dim(trail, half, 1, keepdims=False)
    away = lax.dynamic_index_in_dim(trail, 1 - half, 1, keepdims=False)
    side_top, side_low = a[:256, 256:], a[256:512, 256:]
    small = pltpu.VMEM((256, 256), F32)

    (w11,) = call(
        kernel_a1,
        "panel_a1",
        20_000_000_000,
        q0,
        (jax.ShapeDtypeStruct((256, 256), F32),),
        [quarter, small, block, rows_t],
    )
    w11, q12, away, side_top, side_low = lax.optimization_barrier((w11, q12, away, side_top, side_low))
    q1, q2 = x_swap(q12[:, : 2 * BLK]), q12[:, 2 * BLK :]
    far, low_y = swap(away, 4), swap(side_low, 8)
    side_top = lax.all_gather(side_top, "tile", axis=0, axis_index_groups=z_groups)
    wa, top0 = call(
        kernel_a2, "panel_a2", 20_000_000_000, q0 + [w11], (mid, top_shape), [quarter, small, small, block, rows_t]
    )
    wa, q2, q3, far, low_y, *q1 = lax.optimization_barrier((wa, q2, q3, far, low_y, *q1))
    q2 = x_swap(q2)
    q3_y, q3_z = swap(q3, 8), swap(q3, 16)
    w0hi, w0lo, top1 = call(
        kernel_b,
        "panel_b",
        32_000_000_000,
        q1 + [wa],
        (big, big, top_shape),
        [quarter, quarter, quarter, piece, piece, line, block, rows_t],
    )
    w0hi, far, q3_y, side_top, *q2 = lax.optimization_barrier((w0hi, far, q3_y, side_top, *q2))
    q3 = [q3, q3_y, q3_z, swap(q3_y, 16)]
    both = jnp.concatenate([near, far], 2).reshape(2, 4, 96, 512)
    pieces = [
        lax.dynamic_index_in_dim(both, (col % 4) ^ k, 1, keepdims=False).reshape(192, 512) for k in range(4)
    ]
    pieces = pieces[:1] + [swap(pieces[k], k) for k in range(1, 4)]
    top_y = swap(side_top, 8)
    low_c, wc, top2 = call(
        kernel_c,
        "panel_c",
        35_000_000_000,
        q2 + [w0hi, w0lo],
        (wide, mid, top_shape),
        [quarter, strip, strip, pltpu.VMEM((BLK, 512), F32), block, rows_t],
    )
    wc, top_y, *rest = lax.optimization_barrier((wc, top_y, *pieces, *q3))
    pieces, q3 = rest[:4], rest[4:]
    low_z = [swap(x, 16) for x in (side_low, low_y)]
    sub = jax.ShapeDtypeStruct((2, 96, 1024), BF16)
    (first,) = call(
        functools.partial(rows_kernel, 0),
        "first_rows",
        1_200_000_000,
        pieces + [w0hi, w0lo],
        (sub,),
        [pltpu.VMEM((192, 1024), F32)],
    )
    l0 = lax.all_gather(first, "tile", axis=0, axis_index_groups=row_groups)
    low_d, w1hi, w1lo, top3 = call(
        kernel_d,
        "panel_d",
        38_000_000_000,
        q3 + [w0hi, w0lo, low_c, wc],
        (wide, big, big, top_shape),
        [quarter, quarter, quarter, piece, piece, strip, strip, line, block, rows_t],
    )
    w1hi, *low_z = lax.optimization_barrier((w1hi, *low_z))
    (second,) = call(
        functools.partial(rows_kernel, 1),
        "second_rows",
        1_700_000_000,
        pieces + [w1hi, w1lo, low_c, low_d, first],
        (sub,),
        [pltpu.VMEM((192, 1024), F32)],
    )
    pair = swap(second, 4)
    tall = jax.ShapeDtypeStruct((1024, 768), BF16)
    second, side_top = lax.optimization_barrier((second, side_top))
    t0, nhi, nlo = call(
        columns_first,
        "columns_first",
        9_000_000_000,
        [side_top, top_y, side_low, low_y, *low_z, w0hi, w0lo, low_c, low_d],
        (tall, tall, tall),
        [pltpu.VMEM((1024, 768), BF16)] * 2 + [pltpu.VMEM((1024, 768), F32)],
    )
    nhi, pair = lax.optimization_barrier((nhi, pair))
    later = jnp.stack([second[1], pair[1]])
    l1 = x_swap(jnp.stack([second[0], pair[0]]))
    (t1,) = call(
        columns_second, "columns_second", 9_000_000_000, [nhi, nlo, w1hi, w1lo], (tall,), []
    )
    l1 = [l1]

    def update(h):
        def rows_of(k):
            return pl.BlockSpec((256, 256), lambda j: (2 + 3 * h + k, 1 + j))

        return pl.pallas_call(
            update_kernel,
            grid=(3,),
            out_shape=(
                jax.ShapeDtypeStruct((768, 768), BF16),
                jax.ShapeDtypeStruct((768, 256), BF16),
            ),
            in_specs=[
                pl.BlockSpec((8, 1, 96, 1024), lambda j: (0, h, 0, 0)),
                *[pl.BlockSpec((2, 96, 1024), lambda j: (0, 0, 0))] * 4,
                pl.BlockSpec((1024, 256), lambda j: (0, j)),
                pl.BlockSpec((1024, 256), lambda j: (0, j)),
                rows_of(0),
                rows_of(1),
                rows_of(2),
            ],
            out_specs=(
                pl.BlockSpec((768, 256), lambda j: (0, j)),
                pl.BlockSpec((768, 256), lambda j: (0, 0)),
            ),
            scratch_shapes=[pltpu.VMEM((768, 1024), BF16)],
            compiler_params=PARAMS,
            cost_estimate=cost(2_500_000_000, 9_000_000),
            name="update",
        )(l0, *l1[h], t0, t1, a, a, a)

    children, lower = [], []
    for h in range(2):
        if h:
            across, *l1[1] = lax.optimization_barrier((across, *l1[1]))
            children[0] = (*children[0][:2], across, core_swap(across))
        own, below = update(h)
        if not h:
            own, later = lax.optimization_barrier((own, later))
            l1.append(x_swap(later))
        across = cross(own)
        children.append((own, core_swap(own), across, core_swap(across)))
        lower.append(below)
    factor = jnp.concatenate([top0, top1, top2, top3, *lower], 0)

    column = pl.BlockSpec((2048, 2 * BLK), lambda i, owner, block_map: (0, i))
    merged = pl.pallas_call(
        merge_kernel,
        grid_spec=pltpu.PrefetchScalarGridSpec(
            num_scalar_prefetch=2,
            grid=(4,),
            in_specs=[column] + [pl.BlockSpec(memory_space=pl.ANY)] * 8,
            out_specs=column,
            scratch_shapes=[pltpu.VMEM((4, 1536, 768), BF16), pltpu.SemaphoreType.DMA((4, 2))],
        ),
        out_shape=jax.ShapeDtypeStruct((2048, 1024), F32),
        compiler_params=PARAMS,
        cost_estimate=cost(10_000_000, 22_000_000),
        name="merge",
    )(parent_of, block_map, parents[0, 0], *[children[h][k] for k in range(4) for h in range(2)])
    return factor[None, None], merged[None, None]


def solution(mesh):
    return jax.shard_map(
        per_device,
        mesh=mesh,
        in_specs=(P("front", "tile", None, None), P("front", "tile", None, None), P(), P()),
        out_specs=(P("front", "tile", None, None), P("front", "tile", None, None)),
        check_vma=False,
    )
```

```python
import functools

import jax
import jax.numpy as jnp
from jax import lax
from jax.experimental import pallas as pl
from jax.experimental.pallas import tpu as pltpu
from jax.sharding import PartitionSpec as P

BLK = 128
F32 = jnp.float32
BF16 = jnp.bfloat16
NN = (((1,), (0,)), ((), ()))
NT = (((1,), (1,)), ((), ()))


def dot(a, b, dims):
    return lax.dot_general(a, b, dims, preferred_element_type=F32)


def split(x):
    hi = x.astype(BF16)
    return hi, (x - hi.astype(F32)).astype(BF16)


def dot3(a, b, dims):
    return dot(a[0], b[0], dims) + (dot(a[0], b[1], dims) + dot(a[1], b[0], dims))


def dotp(a, b, dims):
    return dot3(split(a), split(b), dims)


def lane_of(x, lane):
    return jnp.broadcast_to(x[:, lane : lane + 1], (8, BLK))


def factor_block(rows, out_ref, out_row, out_col, T):
    S = list(rows)
    lanes = lax.broadcasted_iota(jnp.int32, (8, BLK), 1)
    subs = lax.broadcasted_iota(jnp.int32, (8, BLK), 0)
    G = [(lanes == subs + 8 * v).astype(F32) for v in range(16)]
    for v0 in range(16):
        far = v0 + 3 + (v0 + 3) % 2
        far = far if far <= 12 else 16
        C = {v: [lane_of(S[v], 8 * v0 + j) for j in range(8)] for v in range(v0, far)}
        at = 80 * (v0 % 2)
        for n, x in enumerate([*C[v0], S[v0], G[v0]]):
            T[at + 8 * n : at + 8 * n + 8, :] = x

        def spread_row(n, i):
            return T[pl.ds(at + 8 * n + i, 8, stride=0), :]

        d = [[spread_row(j, i) if i >= j else None for j in range(8)] for i in range(8)]
        Rs = [spread_row(8, i) for i in range(8)]
        Rg = [spread_row(9, i) for i in range(8)]
        Cn = list(C[v0 + 1]) if v0 < 15 else None
        m = [[None] * 8 for _ in range(8)]
        Us, Ug = [None] * 8, [None] * 8
        wrows = None
        for j in range(8):
            rs = lax.rsqrt(d[j][j])
            p = rs * rs
            w = Rg[j] * rs
            wrows = w if j == 0 else jnp.where(subs == j, w, wrows)
            for i in range(j + 1, 8):
                m[i][j] = d[i][j] * p
            for i in range(j + 1, 8):
                for k in range(j + 1, i + 1):
                    d[i][k] = d[i][k] - m[i][j] * d[k][j]
            Us[j] = Rs[j] * p
            Ug[j] = Rg[j] * p
            if Cn is not None:
                S[v0 + 1] = S[v0 + 1] - Cn[j] * Us[j]
                G[v0 + 1] = G[v0 + 1] - Cn[j] * Ug[j]
            for i in range(j + 1, 8):
                Rs[i] = Rs[i] - m[i][j] * Rs[j]
                Rg[i] = Rg[i] - m[i][j] * Rg[j]
                if Cn is not None:
                    Cn[i] = Cn[i] - m[i][j] * Cn[j]
        out_ref[pl.ds(out_row + 8 * v0, 8), pl.ds(out_col, BLK)] = wrows
        if v0 < 14:
            for j in range(6, -1, -1):
                for i in range(j + 1, 8):
                    Us[j] = Us[j] - m[i][j] * Us[i]
                    Ug[j] = Ug[j] - m[i][j] * Ug[i]
            for v in range(v0 + 2, far):
                for j in range(8):
                    S[v] = S[v] - C[v][j] * Us[j]
                    G[v] = G[v] - C[v][j] * Ug[j]
            if far < 16:
                us, ug = Us[0], Ug[0]
                for j in range(1, 8):
                    us = jnp.where(subs == j, Us[j], us)
                    ug = jnp.where(subs == j, Ug[j], ug)
                parts = [jnp.concatenate([us, ug], 1)]
                if v0:
                    parts.insert(0, jnp.zeros((8 * v0, 2 * BLK), F32))
                parts.append(jnp.zeros((BLK - 8 * v0 - 8, 2 * BLK), F32))
                rank = split(jnp.concatenate(parts, 0))
                less = dot3(split(jnp.concatenate(S[far:], 0)), rank, NN)
                for v in range(far, 16):
                    at = slice(8 * (v - far), 8 * (v - far + 1))
                    S[v] = S[v] - less[at, :BLK]
                    G[v] = G[v] - less[at, BLK:]


def chol_inverse(A, W, Ls, T):
    pairs = A.shape[0] // 256
    W[...] = jnp.zeros(W.shape, F32)

    def step(kb, _):
        r0 = pl.multiple_of(kb * BLK, BLK)
        rows = [A[pl.ds(pl.multiple_of(r0 + 8 * v, 8), 8), pl.ds(r0, BLK)] for v in range(16)]
        factor_block(rows, W, r0, r0, T)

        @pl.when(kb % 2 == 0)
        def _():
            r1 = pl.multiple_of(r0 + BLK, BLK)
            low = dot3(split(A[pl.ds(r1, BLK), pl.ds(r0, BLK)]), split(W[pl.ds(r0, BLK), pl.ds(r0, BLK)]), NT)
            Ls[...] = low
            low = split(low)
            A[pl.ds(r1, BLK), pl.ds(r1, BLK)] -= dot3(low, low, NT)

        @pl.when(kb % 2 == 1)
        def _():
            q = pl.multiple_of(r0 - BLK, BLK)
            t = dot3(split(Ls[...]), split(W[pl.ds(q, BLK), pl.ds(q, BLK)]), NN)
            W[pl.ds(r0, BLK), pl.ds(q, BLK)] = -dot3(split(W[pl.ds(r0, BLK), pl.ds(r0, BLK)]), split(t), NN)

        for c in range(pairs):
            @pl.when(kb == 2 * c + 1)
            def _():
                lo, hi = 256 * c, 256 * (c + 1)
                wd = split(W[lo:hi, lo:hi])
                if c > 0:
                    W[lo:hi, :lo] = dot3(wd, split(W[lo:hi, :lo]), NN)
                if c < pairs - 1:
                    low = split(dot3(split(A[hi:, lo:hi]), wd, NT))
                    for n in range(c + 1, pairs):
                        a, b = 256 * n, 256 * (n + 1)
                        A[a:, a:b] -= dot3([x[a - hi :] for x in low], [x[a - hi : b - hi] for x in low], NT)
                    W[hi:, lo:hi] = -dot3(low, wd, NN)
                    if c > 0:
                        W[hi:, :lo] -= dot3(low, split(W[lo:hi, :lo]), NN)

        return 0

    lax.fori_loop(0, 2 * pairs, step, 0)


VMEM = pl.BlockSpec(memory_space=pltpu.VMEM)
PARAMS = pltpu.CompilerParams(vmem_limit_bytes=56 * 2**20)


def cost(flops, data):
    return pl.CostEstimate(flops=flops, bytes_accessed=data, transcendentals=0)


def position():
    tile = lax.axis_index("tile")
    return tile // 8, tile % 8


def times_inverse_t(x, w, put):
    for n in range(4):
        a, b = 256 * n, 256 * (n + 1)
        put(n, dot3((x[0][:, :b], x[1][:, :b]), (w[0][a:b, :b], w[1][a:b, :b]), NT))


def inverse_times(w, x, put):
    for n in range(4):
        a, b = 256 * n, 256 * (n + 1)
        put(n, dot3((w[0][a:b, :b], w[1][a:b, :b]), (x[0][:b], x[1][:b]), NN))


def store_split(hi, lo, index, x):
    h, l = split(x)
    hi[index] = h
    lo[index] = l


def block_at(index):
    return pl.ds(pl.multiple_of(index * BLK, BLK), BLK)


def finish_lower(whi, wlo, wa, low, wb):
    first, last = split(wa[...]), split(wb[...])
    below = split(-dot3(last, split(dot3(low, first, NN)), NN))
    for out, d0, d1, x in zip((whi, wlo), first, last, below):
        out[:512, :512] = d0
        out[:512, 512:] = jnp.zeros((512, 512), BF16)
        out[512:, :512] = x
        out[512:, 512:] = d1


def own_part(left, whi, wlo, index):
    return dot3(split(left), (whi[block_at(index), :], wlo[block_at(index), :]), NT)


def gather_first(pieces, row, col, A):
    for k in range(4):
        for n in range(4):
            A[block_at(((row ^ n) + 3) % 4), block_at((col % 4) ^ k)] = pieces[k][n * BLK : (n + 1) * BLK, :]


def kernel_a1(*refs):
    pieces = refs[:4]
    w, A, first, Ls, T = refs[4:]
    row, col = position()
    gather_first(pieces, row, col, A)
    first[...] = A[:256, :256]
    chol_inverse(first, w, Ls, T)


def kernel_a2(*refs):
    pieces = refs[:4]
    w, wa, top, A, last, wl, Ls, T = refs[4:]
    row, col = position()
    here = (row + 3) % 4
    gather_first(pieces, row, col, A)
    w11 = split(w[...])
    low = split(dot3(split(A[256:, :256]), w11, NT))
    last[...] = A[256:, 256:] - dot3(low, low, NT)
    chol_inverse(last, wl, Ls, T)
    wa[:256, :256] = w[...]
    wa[:256, 256:] = jnp.zeros((256, 256), F32)
    wa[256:, :256] = -dot3(split(wl[...]), split(dot3(low, w11, NN)), NN)
    wa[256:, 256:] = wl[...]
    own = dotp(A[block_at(here), :], wa[block_at(col % 4), :], NT)
    top[:, :BLK] = jnp.where((col < 4) & (here >= col), own, 0.0).astype(BF16)
    top[:, BLK:] = jnp.zeros((BLK, BLK), BF16)


def kernel_b(*refs):
    pieces = refs[:4]
    wa, whi, wlo, top, D, A, wb, lhi, llo, keep, Ls, T = refs[4:]
    row, col = position()
    here = (row + 3) % 4
    for k in range(4):
        for n in range(4):
            at = block_at(((row ^ n) + 3) % 4), block_at((col % 4) ^ k)
            D[at] = pieces[k][n * BLK : (n + 1) * BLK, :BLK]
            A[at] = pieces[k][n * BLK : (n + 1) * BLK, BLK:]
    keep[:, :512] = D[block_at(here), :]
    keep[:, 512:] = A[block_at(here), :]
    low = split(dot3(split(D[...]), split(wa[...]), NT))
    lhi[...], llo[...] = low
    A[...] -= dot3(low, low, NT)
    chol_inverse(A, wb, Ls, T)
    finish_lower(whi, wlo, wa, (lhi[...], llo[...]), wb)
    own = own_part(keep[...], whi, wlo, col)
    top[:, :BLK] = jnp.where(here + 4 >= col, own, 0.0).astype(BF16)
    top[:, BLK:] = jnp.zeros((BLK, BLK), BF16)


def place(src, i, x, xhi, xlo, blocks):
    rows = block_at(i)
    for half in range(2):
        store_split(xhi, xlo, (rows, block_at(4 * half + x)), src[:, half * BLK : (half + 1) * BLK])
    for n, ref in enumerate(blocks):
        ref[rows, block_at(x)] = src[:, (n + 2) * BLK : (n + 3) * BLK]


def spread(pieces, row, xhi, xlo, blocks):
    for k in range(4):
        for x in range(4):
            place(pieces[k][x], ((row ^ k) + 3) % 4, x, xhi, xlo, blocks)


def kernel_c(*refs):
    pieces = refs[:4]
    w0hi, w0lo, low, wc, top, A, xhi, xlo, keep, Ls, T = refs[4:]
    row, col = position()
    here = (row + 3) % 4
    for k in range(4):
        for n in range(4):
            place(pieces[k][n * BLK : (n + 1) * BLK, :], ((row ^ n) + 3) % 4, (col % 4) ^ k, xhi, xlo, [A])

    def put(n, x):
        low[:, 256 * n : 256 * (n + 1)] = x.astype(BF16)

    times_inverse_t((xhi, xlo), (w0hi, w0lo), put)
    A[...] -= dot(low[...], low[...], NT)
    keep[...] = A[block_at(here), :]
    chol_inverse(A, wc, Ls, T)
    own = dotp(keep[...], wc[block_at(col % 4), :], NT)
    top[:, :BLK] = low[block_at(here), block_at(col)]
    top[:, BLK:] = jnp.where((col < 4) & (here >= col), own, 0.0).astype(BF16)


def kernel_d(*refs):
    pieces = refs[:4]
    w0hi, w0lo, lowc, wc, low, whi, wlo, top, D, A, wd, lhi, llo, xhi, xlo, keep, Ls, T = refs[4:]
    row, col = position()
    here = (row + 3) % 4
    spread(pieces, row, xhi, xlo, [D, A])

    def put(n, x):
        low[:, 256 * n : 256 * (n + 1)] = x.astype(BF16)

    times_inverse_t((xhi, xlo), (w0hi, w0lo), put)
    D[...] -= dot(low[...], lowc[...], NT)
    A[...] -= dot(low[...], low[...], NT)
    keep[:, :512] = D[block_at(here), :]
    keep[:, 512:] = A[block_at(here), :]
    lower = split(dot3(split(D[...]), split(wc[...]), NT))
    lhi[...], llo[...] = lower
    A[...] -= dot3(lower, lower, NT)
    chol_inverse(A, wd, Ls, T)
    finish_lower(whi, wlo, wc, (lhi[...], llo[...]), wd)
    own = own_part(keep[...], whi, wlo, col)
    top[:, :BLK] = low[block_at(here), block_at(col)]
    top[:, BLK:] = jnp.where(here + 4 >= col, own, 0.0).astype(BF16)


def rows_kernel(panel, *refs):
    pieces, refs = refs[:4], refs[4:]
    row, col = position()
    if panel == 0:
        whi, wlo, out, x = refs
    else:
        whi, wlo, low_c, low_d, first, out, x = refs
    for k in range(4):
        for n in range(2):
            at = (2 * n + panel) * BLK
            x[:, block_at(col ^ k ^ (4 * n))] = pieces[k][:, at : at + BLK]
    v = x[...]
    if panel == 1:
        v = v - jnp.concatenate([dot(first[...].reshape(192, 1024), low[...], NT) for low in (low_c, low_d)], 1)

    def put(n, y):
        for h in range(2):
            out[h, :, 256 * n : 256 * (n + 1)] = y[96 * h : 96 * (h + 1)].astype(BF16)

    times_inverse_t(split(v), (whi, wlo), put)


def columns_first(*refs):
    tops, top_y, low_y, low_z = refs[:4]
    w0hi, w0lo, low_c, low_d, t0, nhi, nlo, xhi, xlo, y = refs[4:]
    row, _ = position()
    for n in range(2):
        for top, flip in ((tops, 2 * n), (top_y, 2 * n + 1)):
            at = ((row ^ flip) + 3) % 4
            for m in range(2):
                store_split(xhi, xlo, (block_at(4 * m + at), slice(None)), top[n, m * BLK : (m + 1) * BLK, :])
        for low, z in ((low_y, row // 2), (low_z, 1 - row // 2)):
            at = (2 * z + n + 3) % 4
            for m in range(2):
                y[block_at(4 * m + at), :] = low[n, m * BLK : (m + 1) * BLK, :]

    def put(n, v):
        t0[256 * n : 256 * (n + 1), :] = v.astype(BF16)

    inverse_times((w0hi, w0lo), (xhi, xlo), put)
    for n in range(2):
        at = slice(512 * n, 512 * (n + 1)), slice(None)
        store_split(nhi, nlo, at, y[at] - dot((low_c, low_d)[n][...], t0[...], NN))


def columns_second(nhi, nlo, whi, wlo, t1):
    def put(n, v):
        t1[256 * n : 256 * (n + 1), :] = v.astype(BF16)

    inverse_times((whi, wlo), (nhi, nlo), put)


def update_kernel(l0, *refs):
    pieces, (t0, t1, a0, a1, a2, out, factor, l1) = refs[:4], refs[4:]
    _, col = position()

    @pl.when(pl.program_id(0) == 0)
    def _():
        for k in range(4):
            for n in range(2):
                l1[pl.ds(pl.multiple_of((col ^ k ^ (4 * n)) * 96, 32), 96), :] = pieces[k][n]
        at = block_at(col)
        factor[:, :BLK] = l0[:, 0, :, at].reshape(768, BLK)
        factor[:, BLK:] = l1[:, at]

    total = dot(l0[:, 0].reshape(768, 1024), t0[...], NN) + dot(l1[...], t1[...], NN)
    for n, a in enumerate((a0, a1, a2)):
        at = slice(256 * n, 256 * (n + 1))
        out[at, :] = (a[...] - total[at]).astype(BF16)


def merge_kernel(owner, block_map, parent, *refs):
    children, (out, held, sem) = refs[:8], refs[8:]
    step = pl.program_id(0)
    me = lax.axis_index("front")
    row, col = position()
    here = (row + 3) % 4

    def copies(k):
        return [
            pltpu.make_async_copy(children[2 * k + h], held.at[k, pl.ds(768 * h, 768), :], sem.at[k, h])
            for h in range(2)
        ]

    for k in range(4):
        @pl.when((step == 0) & (owner[me ^ k] == me))
        def _():
            for copy in copies(k):
                copy.start()

    out[...] = parent[...].astype(F32)

    for k in range(4):
        @pl.when((step == 0) & (owner[me ^ k] == me))
        def _():
            for copy in copies(k):
                copy.wait()

    for k in range(4):
        @pl.when(owner[me ^ k] == me)
        def _():
            for b in range(6):
                j = block_map[me ^ k, 8 * b + col] >> 3

                @pl.when(j >> 1 == step)
                def _():
                    for a in range(12):
                        i = block_map[me ^ k, 4 * a + here] >> 2
                        x = held[k, a * BLK : (a + 1) * BLK, b * BLK : (b + 1) * BLK]
                        out[block_at(i), block_at(j & 1)] += x.astype(F32)


def per_device(fronts, parents, parent_of, block_map):
    tile = lax.axis_index("tile")
    row, col = tile // 8, tile % 8
    a = fronts[0, 0]
    big = jax.ShapeDtypeStruct((1024, 1024), BF16)
    mid = jax.ShapeDtypeStruct((512, 512), F32)
    wide = jax.ShapeDtypeStruct((512, 1024), BF16)
    top_shape = jax.ShapeDtypeStruct((BLK, 256), BF16)
    piece = pltpu.VMEM((512, 512), BF16)
    quarter = pltpu.VMEM((512, 512), F32)
    strip = pltpu.VMEM((512, 1024), BF16)
    line = pltpu.VMEM((BLK, 1024), F32)
    block = pltpu.VMEM((BLK, BLK), F32)
    rows_t = pltpu.VMEM((160, BLK), F32)

    crossing = jnp.sum(jnp.where(parent_of // 2 != jnp.arange(4) // 2, 1 << jnp.arange(4), 0))
    def swap(x, k):
        return lax.ppermute(x, "tile", [(i, i ^ k) for i in range(32)])

    def call(kernel, name, flops, ins, outs, scratch):
        return pl.pallas_call(
            kernel,
            out_shape=outs,
            in_specs=[VMEM] * len(ins),
            out_specs=(VMEM,) * len(outs),
            scratch_shapes=scratch,
            compiler_params=PARAMS,
            cost_estimate=cost(flops, 8_000_000),
            name=name,
        )(*ins)

    def core_swap(x):
        return lax.ppermute(x, "front", [(i, i ^ 1) for i in range(4)])

    def cross(x):
        def branch(mask):
            pairs = [(i, i ^ 2) for i in range(4) if mask >> i & 1]
            return lambda v: lax.ppermute(v, "front", pairs) if pairs else jnp.zeros_like(v)

        return lax.switch(crossing, [branch(mask) for mask in range(16)], x)

    x_groups = [[4 * y + x for x in range(4)] for y in range(8)]
    row_groups = [[8 * r + c for c in range(8)] for r in range(4)]
    y_groups = [[i, i + 8] for i in range(32) if not i & 8]
    low_half = col < 4

    def column_swap(x):
        return jnp.concatenate([x] + [swap(x, 8 * k) for k in range(1, 4)], 0)

    def x_swap(x):
        return [x] + [swap(x, k) for k in range(1, 4)]

    q0 = a[:BLK, :BLK]
    q0 = column_swap(jnp.where(low_half, q0, swap(q0, 4)))
    q0, rest = lax.optimization_barrier((q0, a[BLK:512, :256]))
    q0 = x_swap(q0)
    far = swap(rest, 4)
    lo = jnp.where(low_half, rest, far)
    hi = jnp.where(low_half, far, rest)
    q12 = jnp.concatenate(
        [lo[:BLK, :BLK], hi[:BLK, :BLK], lo[BLK : 2 * BLK, :BLK], hi[BLK : 2 * BLK, :BLK], lo[BLK : 2 * BLK, BLK:]], 1
    )
    q12 = column_swap(q12)
    q3 = jnp.concatenate([lo[2 * BLK :, :BLK], hi[2 * BLK :, :BLK], lo[2 * BLK :, BLK:], hi[2 * BLK :, BLK:]], 1)
    q3 = lax.all_gather(q3, "tile", axis=0, axis_index_groups=x_groups)
    trail = a[512:, :256].reshape(2, 2, 384, 256)
    half = col // 4
    near = lax.dynamic_index_in_dim(trail, half, 1, keepdims=False)
    away = lax.dynamic_index_in_dim(trail, 1 - half, 1, keepdims=False)
    side_top, side_low = a[:256, 256:], a[256:512, 256:]
    small = pltpu.VMEM((256, 256), F32)

    (w11,) = call(
        kernel_a1,
        "panel_a1",
        20_000_000_000,
        q0,
        (jax.ShapeDtypeStruct((256, 256), F32),),
        [quarter, small, block, rows_t],
    )
    w11, q12, away, side_top, side_low = lax.optimization_barrier((w11, q12, away, side_top, side_low))
    q1, q2 = x_swap(q12[:, : 2 * BLK]), q12[:, 2 * BLK :]
    far, top_z = swap(away, 4), swap(side_top, 16)
    low_y = lax.all_gather(side_low, "tile", axis=0, axis_index_groups=y_groups)
    wa, top0 = call(
        kernel_a2, "panel_a2", 20_000_000_000, q0 + [w11], (mid, top_shape), [quarter, small, small, block, rows_t]
    )
    wa, q2, q3, far, top_z, *q1 = lax.optimization_barrier((wa, q2, q3, far, top_z, *q1))
    q2 = x_swap(q2)
    q3_y, q3_z = swap(q3, 8), swap(q3, 16)
    w0hi, w0lo, top1 = call(
        kernel_b,
        "panel_b",
        32_000_000_000,
        q1 + [wa],
        (big, big, top_shape),
        [quarter, quarter, quarter, piece, piece, line, block, rows_t],
    )
    w0hi, far, q3_y, *q2 = lax.optimization_barrier((w0hi, far, q3_y, *q2))
    q3 = [q3, q3_y, q3_z, swap(q3_y, 16)]
    both = jnp.concatenate([near, far], 2).reshape(2, 4, 96, 512)
    pieces = [
        lax.dynamic_index_in_dim(both, (col % 4) ^ k, 1, keepdims=False).reshape(192, 512) for k in range(4)
    ]
    pieces = pieces[:1] + [swap(pieces[k], k) for k in range(1, 4)]
    tops = jnp.stack([side_top, top_z])
    top_y = swap(tops, 8)
    low_c, wc, top2 = call(
        kernel_c,
        "panel_c",
        35_000_000_000,
        q2 + [w0hi, w0lo],
        (wide, mid, top_shape),
        [quarter, strip, strip, pltpu.VMEM((BLK, 512), F32), block, rows_t],
    )
    wc, top_y, low_y, *rest = lax.optimization_barrier((wc, top_y, low_y, *pieces, *q3))
    pieces, q3 = rest[:4], rest[4:]
    low_z = swap(low_y, 16)
    sub = jax.ShapeDtypeStruct((2, 96, 1024), BF16)
    (first,) = call(
        functools.partial(rows_kernel, 0),
        "first_rows",
        1_200_000_000,
        pieces + [w0hi, w0lo],
        (sub,),
        [pltpu.VMEM((192, 1024), F32)],
    )
    l0 = lax.all_gather(first, "tile", axis=0, axis_index_groups=row_groups)
    low_d, w1hi, w1lo, top3 = call(
        kernel_d,
        "panel_d",
        38_000_000_000,
        q3 + [w0hi, w0lo, low_c, wc],
        (wide, big, big, top_shape),
        [quarter, quarter, quarter, piece, piece, strip, strip, line, block, rows_t],
    )
    w1hi, low_z = lax.optimization_barrier((w1hi, low_z))
    (second,) = call(
        functools.partial(rows_kernel, 1),
        "second_rows",
        1_700_000_000,
        pieces + [w1hi, w1lo, low_c, low_d, first],
        (sub,),
        [pltpu.VMEM((192, 1024), F32)],
    )
    pair = swap(second, 4)
    tall = jax.ShapeDtypeStruct((1024, 768), BF16)
    second, tops = lax.optimization_barrier((second, tops))
    t0, nhi, nlo = call(
        columns_first,
        "columns_first",
        9_000_000_000,
        [tops, top_y, low_y, low_z, w0hi, w0lo, low_c, low_d],
        (tall, tall, tall),
        [pltpu.VMEM((1024, 768), BF16)] * 2 + [pltpu.VMEM((1024, 768), F32)],
    )
    nhi, pair = lax.optimization_barrier((nhi, pair))
    later = jnp.stack([second[1], pair[1]])
    l1 = x_swap(jnp.stack([second[0], pair[0]]))
    (t1,) = call(
        columns_second, "columns_second", 9_000_000_000, [nhi, nlo, w1hi, w1lo], (tall,), []
    )
    l1 = [l1]

    def update(h):
        def rows_of(k):
            return pl.BlockSpec((256, 256), lambda j: (2 + 3 * h + k, 1 + j))

        return pl.pallas_call(
            update_kernel,
            grid=(3,),
            out_shape=(
                jax.ShapeDtypeStruct((768, 768), BF16),
                jax.ShapeDtypeStruct((768, 256), BF16),
            ),
            in_specs=[
                pl.BlockSpec((8, 1, 96, 1024), lambda j: (0, h, 0, 0)),
                *[pl.BlockSpec((2, 96, 1024), lambda j: (0, 0, 0))] * 4,
                pl.BlockSpec((1024, 256), lambda j: (0, j)),
                pl.BlockSpec((1024, 256), lambda j: (0, j)),
                rows_of(0),
                rows_of(1),
                rows_of(2),
            ],
            out_specs=(
                pl.BlockSpec((768, 256), lambda j: (0, j)),
                pl.BlockSpec((768, 256), lambda j: (0, 0)),
            ),
            scratch_shapes=[pltpu.VMEM((768, 1024), BF16)],
            compiler_params=PARAMS,
            cost_estimate=cost(2_500_000_000, 9_000_000),
            name="update",
        )(l0, *l1[h], t0, t1, a, a, a)

    children, lower = [], []
    for h in range(2):
        if h:
            across, *l1[1] = lax.optimization_barrier((across, *l1[1]))
            children[0] = (*children[0][:2], across, core_swap(across))
        own, below = update(h)
        if not h:
            own, later = lax.optimization_barrier((own, later))
            l1.append(x_swap(later))
        across = cross(own)
        children.append((own, core_swap(own), across, core_swap(across)))
        lower.append(below)
    factor = jnp.concatenate([top0, top1, top2, top3, *lower], 0)

    column = pl.BlockSpec((2048, 2 * BLK), lambda i, owner, block_map: (0, i))
    merged = pl.pallas_call(
        merge_kernel,
        grid_spec=pltpu.PrefetchScalarGridSpec(
            num_scalar_prefetch=2,
            grid=(4,),
            in_specs=[column] + [pl.BlockSpec(memory_space=pl.ANY)] * 8,
            out_specs=column,
            scratch_shapes=[pltpu.VMEM((4, 1536, 768), BF16), pltpu.SemaphoreType.DMA((4, 2))],
        ),
        out_shape=jax.ShapeDtypeStruct((2048, 1024), F32),
        compiler_params=PARAMS,
        cost_estimate=cost(10_000_000, 22_000_000),
        name="merge",
    )(parent_of, block_map, parents[0, 0], *[children[h][k] for k in range(4) for h in range(2)])
    return factor[None, None], merged[None, None]


def solution(mesh):
    return jax.shard_map(
        per_device,
        mesh=mesh,
        in_specs=(P("front", "tile", None, None), P("front", "tile", None, None), P(), P()),
        out_specs=(P("front", "tile", None, None), P("front", "tile", None, None)),
        check_vma=False,
    )
```
